32 devices in a mesh: row: 4 (over z), col: 8 (over y, x, core).
Axes of the slice: x: 2, y: 2, z: 4, core: 2. Of those that a mesh axis runs over, the one named last changes fastest.
Arguments:
- source_tiles: bfloat16 [4, 8, 1024, 128], P('row', 'col'), may hold values from -6 to 6
- requests: int32 [4, 8, 8, 256], P('row', 'col'), may hold values from 0 to 1023
- stencil: int32 [128, 256, 4], P('row', 'col'), may hold values from 0 to 2047, as said below
- regrid_weight: float32 [128, 256, 4], P('row', 'col'), may hold values from 0.1 to 0.6
- w_in: bfloat16 [3, 3, 64, 128], replicated, may hold values from -0.4375 to 0.4375
- w_enc: bfloat16 [3, 3, 128, 128], replicated, may hold values from -0.3125 to 0.3125
- w_mid_first: bfloat16 [3, 3, 128, 128], replicated, may hold values from -0.3125 to 0.3125
- w_mid_second: bfloat16 [3, 3, 128, 128], replicated, may hold values from -0.3125 to 0.3125
- w_dec_first: bfloat16 [3, 3, 256, 128], replicated, may hold values from -0.21875 to 0.21875
- w_dec_second: bfloat16 [3, 3, 128, 128], replicated, may hold values from -0.3125 to 0.3125
- w_out: bfloat16 [128, 64], replicated, may hold values from -0.75 to 0.75
Outputs:
- forecast: bfloat16 [128, 256, 2, 64], P('row', 'col')
The draws below stay inside these ranges and needn't reach their ends.
Inputs may be any that keep to these rules, and one draw needn't show every extreme that they name: `stencil`: within each device's 32 x 32 block of target cells, every slot 0 to 2047 appears at least once among the entries.
All inputs are finite; a program needn't handle non-finite values.
Results may differ from the reference program's by a relative error of at most 0.017.
Values may be sent and summed in bfloat16 or wider, within the bound.
A program may use at most 64 MiB of HBM per device.

```python
import jax
import jax.numpy as jnp
from jax import lax

FIELDS = 64
CH = 128
K = 4
B = 2
TH = 32
TW = 32
SRC = 1024
CAP = 256
SLOTS = 2048
NY = 128
NX = 256
N_ROW = 4
N_COL = 8


def shuffle_reads(tile_key):
    return jax.random.permutation(tile_key, TH * TW * K).astype(jnp.int32)


def draw_stencil(key, part):
    tile_count = N_ROW * N_COL
    tile_reads = TH * TW * K
    tile_keys = jax.random.split(jax.random.fold_in(key, 11), tile_count)
    slot_order = jax.vmap(shuffle_reads)(tile_keys)
    spare_slots = jax.random.randint(jax.random.fold_in(key, 12), (tile_count, tile_reads), 0, SLOTS, dtype=jnp.int32)
    values = jnp.where(slot_order < SLOTS, slot_order, spare_slots)
    values = values.reshape(N_ROW, N_COL, TH, TW, K)
    values = jnp.transpose(values, (0, 2, 1, 3, 4)).reshape(NY, NX, K)
    return values.astype(jnp.int32)


def touch_ends(values, rng, least, top_value):
    extent = values.shape
    place = [jax.random.randint(jax.random.fold_in(rng, axis), (), 0, extent[axis]) for axis in range(len(extent))]
    values = values.at[tuple(place)].set(least)
    longest = extent.index(max(extent))
    place[longest] = (place[longest] + 1) % extent[longest]
    return values.at[tuple(place)].set(top_value)


def block_levels(stream_key, dims, cuts, smallest, largest):
    factor_of = 1.0
    for dim, parts in cuts:
        steps = jax.random.uniform(jax.random.fold_in(jax.random.fold_in(stream_key, 6), dim), (parts,), jnp.float32, smallest / len(cuts), largest / len(cuts))
        factor_of = factor_of * jnp.repeat(jnp.exp(steps), dims[dim] // parts).reshape((-1,) + (1,) * (len(dims) - 1 - dim))
    return factor_of


def normal_values(own_key, dims, scale, reach, pieces=(), kind=jnp.bfloat16):
    entries = scale * jax.random.normal(own_key, dims, jnp.float32)
    if pieces:
        entries = entries * block_levels(own_key, dims, pieces, -0.22, 0.18)
    return jnp.clip(entries, -reach, reach).astype(kind)


def setup_inputs(seed: int = 0) -> dict:
    seeds = jax.random.split(jax.random.key(seed), 12)
    return {
        "source_tiles": normal_values(seeds[0], (N_ROW, N_COL, SRC, B * FIELDS), 1.0, 6.0, ((0, 4), (1, 8))),
        "requests": touch_ends(jax.random.randint(seeds[1], (N_ROW, N_COL, N_COL, CAP), 0, SRC), jax.random.fold_in(seeds[1], 1), 0, SRC - 1).astype(jnp.int32),
        "stencil": draw_stencil(jax.random.fold_in(seeds[11], 71), 0),
        "regrid_weight": jnp.clip(0.1 + 0.5 * jax.random.uniform(seeds[3], (NY, NX, K), jnp.float32) ** block_levels(seeds[3], (NY, NX, K), ((0, 4), (1, 8)), -0.2, 0.2), 0.1, 0.6),
        "w_in": normal_values(seeds[4], (3, 3, FIELDS, CH), (3 * FIELDS) ** -0.5, 0.4375),
        "w_enc": normal_values(seeds[5], (3, 3, CH, CH), (3 * CH) ** -0.5, 0.3125),
        "w_mid_first": normal_values(seeds[6], (3, 3, CH, CH), (3 * CH) ** -0.5, 0.3125),
        "w_mid_second": normal_values(seeds[7], (3, 3, CH, CH), (3 * CH) ** -0.5, 0.3125),
        "w_dec_first": normal_values(seeds[8], (3, 3, 2 * CH, CH), (6 * CH) ** -0.5, 0.21875),
        "w_dec_second": normal_values(seeds[9], (3, 3, CH, CH), (3 * CH) ** -0.5, 0.3125),
        "w_out": normal_values(seeds[10], (CH, FIELDS), (CH // 2) ** -0.5, 0.75),
    }


def conv_same(values, weight):
    padded = jnp.pad(values, ((0, 0), (1, 1), (0, 0), (0, 0)), mode="wrap")
    padded = jnp.pad(padded, ((1, 1), (0, 0), (0, 0), (0, 0)))
    inputs = jnp.transpose(padded, (2, 0, 1, 3)).astype(jnp.float32)
    result = lax.conv_general_dilated(inputs, weight.astype(jnp.float32), (1, 1), "VALID", dimension_numbers=("NHWC", "HWIO", "NHWC"), precision=lax.Precision.HIGHEST)
    return jnp.transpose(result, (1, 2, 0, 3))


def layer(values, weight):
    return jax.nn.silu(conv_same(values, weight)).astype(jnp.bfloat16)


def reference(source_tiles, requests, stencil, regrid_weight, w_in, w_enc, w_mid_first, w_mid_second, w_dec_first, w_dec_second, w_out):
    def band_rows(block):
        tiles_band = source_tiles[block]
        wanted = requests[block]
        senders = jnp.arange(N_COL, dtype=jnp.int32)[None, :, None]
        buffer = tiles_band[senders, wanted]
        flattened = buffer.reshape(N_COL * SLOTS, B * FIELDS)
        start = (block * TH).astype(jnp.int32)
        band_stencil = lax.dynamic_slice_in_dim(stencil, start, TH, 0)
        band_weight = lax.dynamic_slice_in_dim(regrid_weight, start, TH, 0)
        owner = (jnp.arange(NX, dtype=jnp.int32) // TW)[None, :, None]
        picked = flattened[owner * SLOTS + band_stencil]
        total = jnp.sum(picked.astype(jnp.float32) * band_weight[..., None], axis=2)
        return total.astype(jnp.bfloat16)

    bands = lax.map(band_rows, jnp.arange(N_ROW, dtype=jnp.int32))
    regridded = bands.reshape(NY, NX, B, FIELDS)
    first = layer(regridded, w_in)
    skip = layer(first, w_enc)
    pooled = skip.astype(jnp.float32).reshape(NY // 2, 2, NX // 2, 2, B, CH).mean(axis=(1, 3)).astype(jnp.bfloat16)
    middle = layer(pooled, w_mid_first)
    coarse = layer(middle, w_mid_second)
    upsampled = jnp.repeat(jnp.repeat(coarse, 2, axis=0), 2, axis=1)
    joined = jnp.concatenate([upsampled, skip], axis=-1)
    decoded = layer(layer(joined, w_dec_first), w_dec_second)
    result = jnp.dot(decoded.reshape(-1, CH), w_out, preferred_element_type=jnp.float32)
    return result.reshape(NY, NX, B, FIELDS).astype(jnp.bfloat16)
```

```python
import functools

import jax
import jax.numpy as jnp
from jax import lax
from jax.experimental import pallas as pl
from jax.experimental.pallas import tpu as pltpu
from jax.sharding import PartitionSpec as P

FIELDS = 64
CH = 128
HALO = 8


def silu(a):
    return a * (0.5 + 0.5 * jnp.tanh(0.5 * a))


def unet_kernel(
    tile_rows, tile_cols, p_ref, w_in, w_enc, w_m1, w_m2, w_d1, w_d2, w_out, out_ref,
    first, skip, pooled, middle, up, dec1, tmp, c_in, c_enc, c_m1, c_m2, c_d1, c_d2, c_out, pairs,
):
    wide = tile_cols + 2 * HALO
    half = wide // 2
    row = lax.axis_index("row")
    at_top = row == 0
    at_bottom = row == lax.axis_size("row") - 1
    f32, bf16 = jnp.float32, jnp.bfloat16

    c_in[...] = jnp.zeros_like(c_in)
    c_out[...] = jnp.zeros_like(c_out)
    w_last = w_out[...].astype(f32).T.astype(bf16)
    for b in range(2):
        c_out[b * CH : (b + 1) * CH, b * FIELDS : (b + 1) * FIELDS] = w_last
    size = p_ref.shape[0]
    values = p_ref[...].astype(f32)
    turned = pltpu.roll(values, FIELDS, 1)
    below = pltpu.roll(values, size - wide, 0)
    turned_below = pltpu.roll(turned, size - wide, 0)
    low = lax.broadcasted_iota(jnp.int32, (size, CH), 1) < FIELDS
    pairs[0] = jnp.where(low, values, turned_below).astype(bf16)
    pairs[1] = jnp.where(low, turned, below).astype(bf16)
    for dy in range(3):
        for dx in range(3):
            rows = slice(dy * CH, (dy + 1) * CH)
            cols = slice(dx * CH, (dx + 1) * CH)
            c_in[dy * FIELDS : (dy + 1) * FIELDS, cols] = w_in[dy, dx]
            c_enc[rows, cols] = w_enc[dy, dx]
            c_m1[rows, cols] = w_m1[dy, dx]
            c_m2[rows, cols] = w_m2[dy, dx]
            c_d1[rows, cols] = w_d1[dy, dx, :CH]
            c_d1[(dy + 3) * CH : (dy + 4) * CH, cols] = w_d1[dy, dx, CH:]
            c_d2[rows, cols] = w_d2[dy, dx]

    def conv(sources, weight, width, chunk_rows, start, steps=(0, 1, 2)):
        size = chunk_rows * width
        windows = [
            load(pl.multiple_of(start + (offset + dy) * width, 8), size).astype(bf16)
            for load, offset in sources
            for dy in steps
        ]
        u = jnp.dot(jnp.concatenate(windows, axis=1), weight[...], preferred_element_type=f32)
        return silu(
            u[:, CH : 2 * CH]
            + pltpu.roll(u[:, :CH], 1, 0)
            + pltpu.roll(u[:, 2 * CH :], size - 1, 0)
        )

    def per_chunk(height, chunk_rows, width, step):
        chunks = height // chunk_rows

        @pl.loop(0, 2 * chunks)
        def _(i):
            b = i // chunks
            start = pl.multiple_of((i % chunks) * (chunk_rows * width), 8)
            step(b, start)

    def clear(ref, depth, inner, width):
        @pl.when(at_top)
        def _():
            ref[:, : depth * width] = jnp.zeros((2, depth * width, CH), ref.dtype)

        @pl.when(at_bottom)
        def _():
            ref[:, (depth + inner) * width :] = jnp.zeros((2, depth * width, CH), ref.dtype)

    def reader(ref, b):
        return lambda start, size: ref[b, pl.ds(start, size), :]

    h_first = tile_rows + 14
    h_skip = tile_rows + 12
    h_pool = h_skip // 2
    h_mid = h_pool - 2
    h_coarse = h_mid - 2
    h_dec1 = tile_rows + 2

    def first_step(b, start):
        chunk = h_first // 2
        value = conv([(reader(pairs, b), 0)], c_in, wide, chunk, start, (0, 2))
        first[b, pl.ds(start, chunk * wide), :] = value.astype(bf16)

    per_chunk(h_first, h_first // 2, wide, first_step)
    clear(first, 7, tile_rows, wide)

    def skip_step(b, start):
        chunk = h_skip // 2
        value = conv([(reader(first, b), 0)], c_enc, wide, chunk, start)
        skip[b, pl.ds(start, chunk * wide), :] = value.astype(bf16)

    per_chunk(h_skip, h_skip // 2, wide, skip_step)
    clear(skip, 6, tile_rows, wide)

    @pl.loop(0, 2)
    def _(b):
        s = skip[b].astype(f32).reshape(h_pool, 2 * wide, CH)
        tmp[: h_pool * wide, :] = (s[:, :wide] + s[:, wide:]).reshape(h_pool * wide, CH)
        total = (
            tmp[pl.ds(0, h_pool * half, stride=2), :] + tmp[pl.ds(1, h_pool * half, stride=2), :]
        )
        pooled[b] = (total * 0.25).astype(bf16).astype(f32)

    def mid_step(b, start):
        value = conv([(reader(pooled, b), 0)], c_m1, half, h_mid, start)
        middle[b, pl.ds(start, h_mid * half), :] = value.astype(bf16).astype(f32)

    per_chunk(h_mid, h_mid, half, mid_step)
    clear(middle, 2, tile_rows // 2, half)

    @pl.loop(0, 2)
    def _(b):
        value = conv([(reader(middle, b), 0)], c_m2, half, h_coarse, 0)
        size = h_coarse * half
        tmp[pl.ds(0, size, stride=2), :] = value
        tmp[pl.ds(1, size, stride=2), :] = value
        v = tmp[: h_coarse * wide, :].astype(bf16).reshape(h_coarse, 1, wide, CH)
        up[b] = jnp.broadcast_to(v, (h_coarse, 2, wide, CH)).reshape(2 * h_coarse * wide, CH)

    clear(up, 2, tile_rows, wide)

    def dec1_step(b, start):
        chunk = h_dec1 // 2
        value = conv([(reader(up, b), 0), (reader(skip, b), 4)], c_d1, wide, chunk, start)
        dec1[b, pl.ds(start, chunk * wide), :] = value.astype(bf16)

    per_chunk(h_dec1, h_dec1 // 2, wide, dec1_step)
    clear(dec1, 1, tile_rows, wide)

    chunk = tile_rows // 2

    @pl.loop(0, 2)
    def _(i):
        start = pl.multiple_of(i * (chunk * wide), 8)
        both = []
        for b in range(2):
            value = conv([(reader(dec1, b), 0)], c_d2, wide, chunk, start)
            value = value.reshape(chunk, wide, CH)[:, HALO : HALO + tile_cols]
            both.append(value.reshape(chunk * tile_cols, CH).astype(bf16))
        result = jnp.dot(
            jnp.concatenate(both, axis=1), c_out[...], preferred_element_type=f32
        )
        place = pl.multiple_of(i * (chunk * tile_cols), 8)
        out_ref[pl.ds(place, chunk * tile_cols), :] = result.astype(bf16)


def unet_scratch(tile_rows, tile_cols):
    wide = tile_cols + 2 * HALO
    half = wide // 2
    f32, bf16 = jnp.float32, jnp.bfloat16
    square = pltpu.VMEM((3 * CH, 3 * CH), bf16)
    return [
        pltpu.VMEM((2, (tile_rows + 14) * wide, CH), bf16),
        pltpu.VMEM((2, (tile_rows + 12) * wide, CH), bf16),
        pltpu.VMEM((2, (tile_rows // 2 + 6) * half, CH), f32),
        pltpu.VMEM((2, (tile_rows // 2 + 4) * half, CH), f32),
        pltpu.VMEM((2, (tile_rows + 4) * wide, CH), bf16),
        pltpu.VMEM((2, (tile_rows + 2) * wide, CH), bf16),
        pltpu.VMEM(((tile_rows // 2 + 6) * wide, CH), f32),
        pltpu.VMEM((4 * FIELDS, 3 * CH), bf16),
        square, square, square,
        pltpu.VMEM((6 * CH, 3 * CH), bf16),
        square,
        pltpu.VMEM((2 * CH, 2 * FIELDS), bf16),
        pltpu.VMEM((2, (tile_rows + 2 * HALO) * wide, CH), bf16),
    ]


MESH = pl.DeviceIdType.MESH


def whole_kernel(tile_rows, tile_cols, *refs):
    ins, w_hbm, final = refs[:4], refs[4:11], refs[11]
    scratch = refs[12:]
    regrid_scratch, rest = scratch[:20], scratch[20:]
    padded, w_vmem, w_sem, unet_scratch = rest[0], rest[1:8], rest[8], rest[9:]
    copies = [pltpu.make_async_copy(a, b, w_sem.at[i]) for i, (a, b) in enumerate(zip(w_hbm, w_vmem))]
    regrid_kernel(tile_rows, tile_cols, copies, *ins, padded, *regrid_scratch)
    for copy in copies:
        copy.wait()
    unet_kernel(tile_rows, tile_cols, padded, *w_vmem, final, *unet_scratch)


def regrid_kernel(
    tile_rows, tile_cols, weight_copies, src_in, req_in, sten_in, wgt_in, out_ref,
    src_ref, req_ref, sten_ref, wgt_ref, load, reqs, src_t, mix, outbox, inbox, acc, pad, slot_rows, weight_rows,
    req_send, req_recv, box_send, box_recv, halo_send, halo_recv,
):
    f32, bf16 = jnp.float32, jnp.bfloat16
    row, me = lax.axis_index("row"), lax.axis_index("col")
    n_row, n = lax.axis_size("row"), lax.axis_size("col")
    cap = req_ref.shape[1]
    cells = src_ref.shape[0]
    spots = tile_rows * tile_cols
    has_up, has_down = row > 0, row < n_row - 1
    blocks = tile_cols // HALO
    edge = HALO * HALO
    inner = tile_rows * HALO

    loads = [
        pltpu.make_async_copy(outer, held, load.at[i])
        for i, (outer, held) in enumerate(
            [(req_in, req_ref), (src_in, src_ref), (sten_in, sten_ref), (wgt_in, wgt_ref)]
        )
    ]
    for copy in loads:
        copy.start()
    for copy in weight_copies:
        copy.start()

    barrier = pltpu.get_barrier_semaphore()

    def greet(r, c):
        pl.semaphore_signal(
            barrier, inc=1, device_id=(r, lax.rem(c + n, n)), device_id_type=MESH
        )

    @pl.loop(1, n)
    def _(step):
        greet(row, me + step)

    @pl.when(has_up)
    def _():
        for d in (-1, 0, 1):
            greet(row - 1, me + d)

    @pl.when(has_down)
    def _():
        for d in (-1, 0, 1):
            greet(row + 1, me + d)

    rows_beside = jnp.minimum(row, 1) + jnp.minimum(n_row - 1 - row, 1)
    pl.semaphore_wait(barrier, n - 1 + 3 * rows_beside)

    loads[0].wait()

    def ask(step, sender):
        return pltpu.make_async_remote_copy(
            src_ref=req_ref,
            dst_ref=reqs.at[sender],
            send_sem=req_send.at[step],
            recv_sem=req_recv.at[sender],
            device_id=(row, lax.rem(me + step, n)),
            device_id_type=MESH,
        )

    @pl.loop(1, n)
    def _(step):
        ask(step, me).start()

    reqs[me] = req_ref[...]
    loads[1].wait()
    src_t[...] = src_ref[...].astype(f32).T.astype(bf16)

    loads[2].wait()
    loads[3].wait()
    taps = sten_ref.shape[1]
    for k in range(taps):
        slot_rows[k : k + 1, :] = jnp.concatenate(
            [sten_ref[y, k : k + 1, :] for y in range(tile_rows)], axis=1
        ).astype(f32)
        weight_rows[k : k + 1, :] = jnp.concatenate(
            [wgt_ref[y, k : k + 1, :] for y in range(tile_rows)], axis=1
        )
    tile, piece = 16, 256

    def ladder(width):
        return lax.broadcasted_iota(jnp.int32, (tile, width), 0).astype(f32).astype(bf16)

    def spread(values):
        return jnp.broadcast_to(values, (tile, values.shape[1])).astype(bf16)

    lanes = min(512, spots)
    zero, one = jnp.zeros((), bf16), jnp.ones((), bf16)

    def mix_block(j):
        for left_lane in range(0, spots, lanes):
            here = slice(left_lane, left_lane + lanes)
            ids = ladder(lanes)
            weights = [spread(weight_rows[k : k + 1, here]) for k in range(taps)]
            for start in range(0, cap, piece):
                base = (j * cap + start).astype(f32)
                near = [spread(slot_rows[k : k + 1, here] - base) for k in range(taps)]
                for g in range(0, min(piece, cap), tile):
                    step_ids = ids + jnp.asarray(g, bf16)
                    total = None
                    for k in range(taps):
                        part = jnp.where(step_ids == near[k], weights[k], zero)
                        total = part if total is None else total + part
                    mix[j, start + g : start + g + tile, here] = total

    @pl.loop(0, n // 2)
    def _(j):
        mix_block(j)

    def picked(dest):
        asked = reqs[dest, pl.ds(me, 1), :].astype(f32)
        ids = ladder(cap)
        rows = []
        for start in range(0, cells, piece):
            near = spread(asked - float(start))
            for g in range(0, piece, tile):
                rows.append(jnp.where(ids + jnp.asarray(g, bf16) == near, one, zero))
        hot = jnp.concatenate(rows, axis=0)
        return jnp.dot(src_t[...], hot, preferred_element_type=f32).astype(bf16)

    def post(step, sender):
        return pltpu.make_async_remote_copy(
            src_ref=outbox.at[step],
            dst_ref=inbox.at[sender],
            send_sem=box_send.at[step],
            recv_sem=box_recv.at[sender],
            device_id=(row, lax.rem(me + step, n)),
            device_id_type=MESH,
        )

    @pl.loop(1, n)
    def _(step):
        dest = lax.rem(me + step, n)
        ask(step, dest).wait_recv()
        outbox[step] = picked(dest)
        post(step, me).start()

    inbox[me] = picked(me)

    @pl.loop(n // 2, n)
    def _(j):
        mix_block(j)

    acc[...] = jnp.dot(inbox[me], mix[me], preferred_element_type=f32)

    @pl.loop(1, n)
    def _(step):
        sender = lax.rem(me - step + n, n)
        post(step, sender).wait_recv()
        acc[...] += jnp.dot(inbox[sender], mix[sender], preferred_element_type=f32)

    grid = acc[...].T.reshape(tile_rows, blocks, HALO, 2 * FIELDS)
    for xb in range(blocks):
        pad[xb + 1, edge : edge + inner, :] = (
            grid[:, xb].reshape(inner, 2 * FIELDS).astype(bf16)
        )

    @pl.when(jnp.logical_not(has_up))
    def _():
        pad[:, :edge] = jnp.zeros((blocks + 2, edge, 2 * FIELDS), bf16)

    @pl.when(jnp.logical_not(has_down))
    def _():
        pad[:, edge + inner :] = jnp.zeros((blocks + 2, edge, 2 * FIELDS), bf16)

    mid = slice(edge, edge + inner)
    first, last = slice(edge, 2 * edge), slice(inner, inner + edge)
    low, high = slice(0, edge), slice(edge + inner, 2 * edge + inner)
    every = slice(1, blocks + 1)
    left, right = slice(1, 2), slice(blocks, blocks + 1)
    before, after = slice(0, 1), slice(blocks + 1, blocks + 2)
    moves = [
        (0, 1, (right, mid), (before, mid)),
        (0, -1, (left, mid), (after, mid)),
        (1, 0, (every, last), (every, low)),
        (1, 1, (right, last), (before, low)),
        (1, -1, (left, last), (after, low)),
        (-1, 0, (every, first), (every, high)),
        (-1, 1, (right, first), (before, high)),
        (-1, -1, (left, first), (after, high)),
    ]

    def shift(i):
        dr, dc, src, dst = moves[i]
        return pltpu.make_async_remote_copy(
            src_ref=pad.at[src[0], src[1]],
            dst_ref=pad.at[dst[0], dst[1]],
            send_sem=halo_send.at[i],
            recv_sem=halo_recv.at[i],
            device_id=(row + dr, lax.rem(me + dc + n, n)),
            device_id_type=MESH,
        )

    @pl.when(has_down)
    def _():
        for i in (2, 3, 4):
            shift(i).start()

    @pl.when(has_up)
    def _():
        for i in (5, 6, 7):
            shift(i).start()

    for i in (0, 1):
        shift(i).start()
    for i in (0, 1):
        shift(i).wait()

    @pl.when(has_up)
    def _():
        for i in (2, 3, 4):
            shift(i).wait_recv()

    @pl.when(has_down)
    def _():
        for i in (5, 6, 7):
            shift(i).wait_recv()

    parts = [
        pad[xb].astype(f32).reshape(tile_rows + 2 * HALO, HALO, 2 * FIELDS)
        for xb in range(blocks + 2)
    ]
    out_ref[...] = jnp.concatenate(parts, axis=1).reshape(out_ref.shape).astype(bf16)

    @pl.when(has_down)
    def _():
        for i in (2, 3, 4):
            shift(i).wait_send()

    @pl.when(has_up)
    def _():
        for i in (5, 6, 7):
            shift(i).wait_send()

    @pl.loop(1, n)
    def _(step):
        ask(step, me).wait_send()
        post(step, me).wait_send()


def regrid(source, wanted, stencil, weight, weights, tile_rows, tile_cols):
    f32, bf16 = jnp.float32, jnp.bfloat16
    n, cap = wanted.shape
    cells, columns = source.shape
    spots = tile_rows * tile_cols
    blocks = tile_cols // HALO
    rows = tile_rows + 2 * HALO
    dma = pltpu.SemaphoreType.DMA
    return pl.pallas_call(
        functools.partial(whole_kernel, tile_rows, tile_cols),
        out_shape=jax.ShapeDtypeStruct((tile_rows * tile_cols, columns), bf16),
        in_specs=[pl.BlockSpec(memory_space=pltpu.HBM)] * 11,
        out_specs=pl.BlockSpec(memory_space=pltpu.VMEM),
        scratch_shapes=[
            pltpu.VMEM(source.shape, bf16),
            pltpu.VMEM(wanted.shape, jnp.int32),
            pltpu.VMEM(stencil.shape, jnp.int32),
            pltpu.VMEM(weight.shape, f32),
            dma((4,)),
            pltpu.VMEM((n, n, cap), jnp.int32),
            pltpu.VMEM((columns, cells), bf16),
            pltpu.VMEM((n, cap, spots), bf16),
            pltpu.VMEM((n, columns, cap), bf16),
            pltpu.VMEM((n, columns, cap), bf16),
            pltpu.VMEM((columns, spots), f32),
            pltpu.VMEM((blocks + 2, rows * HALO, columns), bf16),
            pltpu.VMEM((stencil.shape[1], spots), f32),
            pltpu.VMEM((stencil.shape[1], spots), f32),
            dma((n,)), dma((n,)), dma((n,)), dma((n,)), dma((8,)), dma((8,)),
            pltpu.VMEM((rows * (tile_cols + 2 * HALO), columns), bf16),
        ] + [pltpu.VMEM(w.shape, bf16) for w in weights] + [dma((7,))] + unet_scratch(tile_rows, tile_cols),
        compiler_params=pltpu.CompilerParams(
            collective_id=0, has_side_effects=True, vmem_limit_bytes=60 * 1024 * 1024
        ),
        cost_estimate=pl.CostEstimate(
            flops=10**9, bytes_accessed=2 * 10**6, transcendentals=0
        ),
    )(source, wanted, stencil, weight, *weights)


def body(source_tiles, requests, stencil, regrid_weight, *weights):
    tile_rows, tile_cols = stencil.shape[:2]
    cells, columns = source_tiles.shape[2:]
    result = regrid(
        source_tiles.reshape(cells, columns),
        requests.reshape(requests.shape[2:]),
        stencil.transpose(0, 2, 1),
        regrid_weight.transpose(0, 2, 1),
        (*weights[:-1], weights[-1].T),
        tile_rows,
        tile_cols,
    )
    return result.reshape(tile_rows, tile_cols, 2, FIELDS)


def solution(mesh):
    placed = (P("row", "col", None, None),) * 2 + (P("row", "col", None),) * 2 + (P(),) * 7
    return jax.shard_map(
        body, mesh=mesh, in_specs=placed, out_specs=P("row", "col", None, None), check_vma=False
    )
```

```python
import functools

import jax
import jax.numpy as jnp
from jax import lax
from jax.experimental import pallas as pl
from jax.experimental.pallas import tpu as pltpu
from jax.sharding import PartitionSpec as P

FIELDS = 64
CH = 128
HALO = 8
f32, bf16 = jnp.float32, jnp.bfloat16
MESH = pl.DeviceIdType.MESH


def silu(a):
    return a * (0.5 + 0.5 * jnp.tanh(0.5 * a))


def pair_weight(out, base, w, dy):
    zero = jnp.zeros((CH, CH), bf16)
    rows = [
        (w[dy, 1], w[dy, 0]), (w[dy, 2], w[dy, 1]), (w[dy, 0], zero), (zero, w[dy, 2])
    ]
    for i, (even, odd) in enumerate(rows):
        place = slice(base + i * CH, base + (i + 1) * CH)
        out[place, :CH] = even
        out[place, CH:] = odd


def prepare(w_in, w_enc, w_m1, w_m2, w_d1, w_d2, w_out, c_in, c_enc, c_m1, c_m2, c_d1, c_d2, c_out):
    quad = 4 * FIELDS
    none = jnp.zeros((FIELDS, CH), bf16)
    for dy in range(3):
        for j in range(4):
            place = slice(dy * quad + j * FIELDS, dy * quad + (j + 1) * FIELDS)
            c_in[place, :CH] = w_in[dy, j] if j < 3 else none
            c_in[place, CH:] = w_in[dy, j - 1] if j > 0 else none
        base = dy * 4 * CH
        pair_weight(c_enc, base, w_enc, dy)
        pair_weight(c_m1, base, w_m1, dy)
        pair_weight(c_m2, base, w_m2, dy)
        pair_weight(c_d2, base, w_d2, dy)
        for par in range(2):
            pair_weight(c_d1.at[par], base, w_d1.at[:, :, CH:], dy)
    zero = jnp.zeros((CH, CH), bf16)
    for par in range(2):
        groups = ((0, 1), (2,)) if par == 0 else ((0,), (1, 2))
        for g, dys in enumerate(groups):
            taps = [sum(w_d1[dy, dx, :CH].astype(f32) for dy in dys) for dx in range(3)]
            base = 12 * CH + g * 3 * CH
            rows = [
                (taps[0].astype(bf16), zero),
                ((taps[1] + taps[2]).astype(bf16), (taps[0] + taps[1]).astype(bf16)),
                (zero, taps[2].astype(bf16)),
            ]
            for i, (even, odd) in enumerate(rows):
                place = slice(base + i * CH, base + (i + 1) * CH)
                c_d1[par, place, :CH] = even
                c_d1[par, place, CH:] = odd
    last = w_out[...].astype(f32).T.astype(bf16)
    pad = jnp.zeros((CH, CH - FIELDS), bf16)
    full = jnp.concatenate([last.astype(f32), pad.astype(f32)], axis=1).astype(bf16)
    c_out[:CH, :CH] = full
    c_out[CH:, CH:] = full
    c_out[:CH, CH:] = zero
    c_out[CH:, :CH] = zero


def pairs_of(tile_cols):
    return tile_cols // 2 + HALO


def unet_body(tile_rows, tile_cols, at_top, at_bottom, pad, weights, out_ref, quad, first, skip, tmp, pooled, middle, up, dec, last):
    c_in, c_enc, c_m1, c_m2, c_d1, c_d2, c_out = weights
    rows = tile_rows + 2 * HALO
    pairs = pairs_of(tile_cols)
    line = 2 * pairs
    half = line // 2
    h_first, h_skip = tile_rows + 14, tile_rows + 12
    h_pool = h_skip // 2
    h_mid, h_coarse = h_pool - 2, h_pool - 4
    h_dec = (tile_rows + 2) // 2
    own = tile_cols // 2
    low = lax.broadcasted_iota(jnp.int32, (1, 1, CH), 2) < FIELDS
    upper = lax.broadcasted_iota(jnp.int32, (1, 8, 1), 1) < 4
    groups = pairs // 8

    def rolled(value, by):
        return pltpu.roll(value, by % value.shape[0], 0)

    def line_up(start, count):
        columns = []
        for par in range(2):
            lanes = slice(par * CH, (par + 1) * CH)
            parts = []
            for g in range(groups):
                place = pl.ds(start * 4, count * 4)
                a = pad[2 * g, place, lanes].astype(f32).reshape(count // 2, 8, CH)
                b = pad[2 * g + 1, place, lanes].astype(f32).reshape(count // 2, 8, CH)
                turned_a, turned_b = pltpu.roll(a, 4, 1), pltpu.roll(b, 4, 1)
                both = jnp.stack(
                    [jnp.where(upper, a, turned_b), jnp.where(upper, turned_a, b)], axis=1
                )
                parts.append(both.reshape(count, 8, CH))
            columns.append(jnp.concatenate(parts, axis=1).reshape(count * pairs, CH))
        even, odd = columns
        even_t, odd_t = pltpu.roll(even, FIELDS, 1), pltpu.roll(odd, FIELDS, 1)
        before, before_t = rolled(odd, 1), rolled(odd_t, 1)
        after, after_t = rolled(even, -1), rolled(even_t, -1)
        lo = low.reshape(1, CH)
        one = [jnp.where(lo, before, even_t), jnp.where(lo, odd, after_t)]
        two = [jnp.where(lo, before_t, even), jnp.where(lo, odd_t, after)]
        both = [
            jnp.concatenate(v, axis=1).reshape(count, pairs, 2 * CH) for v in (one, two)
        ]
        value = jnp.concatenate(both, axis=1).reshape(count * line, 2 * CH).astype(bf16)
        quad[pl.ds(start * line, count * line), :] = value

    step = 16
    @pl.loop(0, rows // step)
    def _(i):
        line_up(pl.multiple_of(i * step, step), step)

    def dot(windows, weight):
        return silu(
            jnp.dot(jnp.concatenate(windows, axis=1), weight, preferred_element_type=f32)
        )

    def sides(value):
        return jnp.concatenate([rolled(value[:, CH:], 1), rolled(value[:, :CH], -1)], axis=1)

    def window(ref, start, count, width, dy):
        return ref[pl.ds(pl.multiple_of((start + dy) * width, 8), count * width), :]

    def clear(ref, depth, inner, width):
        @pl.when(at_top)
        def _():
            ref[: depth * width] = jnp.zeros((depth * width, ref.shape[1]), ref.dtype)

        @pl.when(at_bottom)
        def _():
            ref[(depth + inner) * width :] = jnp.zeros((depth * width, ref.shape[1]), ref.dtype)

    def chunks(total, count, fn):
        if total == count:
            fn(0)
        else:
            @pl.loop(0, total // count)
            def _(i):
                fn(i * count)

    count = h_first // FIRST_CHUNKS

    def first_step(start):
        v = dot([window(quad, start, count, line, dy) for dy in range(3)], c_in[...])
        v = jnp.concatenate([v, sides(v)], axis=1).astype(bf16)
        first[pl.ds(pl.multiple_of(start * line, 16), count * line), :] = v

    chunks(h_first, count, first_step)
    clear(first, 7, tile_rows, line)

    count_s = h_skip // SKIP_CHUNKS

    def skip_step(start):
        v = dot([window(first, start, count_s, line, dy) for dy in range(3)], c_enc[...])
        both = jnp.concatenate([v, sides(v)], axis=1).astype(bf16)
        skip[pl.ds(start // 2, count_s // 2)] = both.reshape(count_s // 2, 2 * line, 4 * CH)
        v = v.reshape(count_s // 2, 2 * line, 2 * CH)
        v = (v[:, :line] + v[:, line:]).reshape(count_s // 2 * line, 2 * CH)
        place = pl.ds(pl.multiple_of(start * line // 2, 8), count_s // 2 * line)
        tmp[place, :] = (v[:, :CH] + v[:, CH:]) * 0.25

    chunks(h_skip, count_s, skip_step)

    @pl.when(at_top)
    def _():
        skip[:3] = jnp.zeros((3, 2 * line, 4 * CH), bf16)

    @pl.when(at_bottom)
    def _():
        skip[h_pool - 3 :] = jnp.zeros((3, 2 * line, 4 * CH), bf16)

    @pl.when(at_top)
    def _():
        tmp[: 3 * line] = jnp.zeros((3 * line, CH), f32)

    @pl.when(at_bottom)
    def _():
        tmp[(h_pool - 3) * line :] = jnp.zeros((3 * line, CH), f32)

    size = h_pool * half
    v = jnp.concatenate([tmp[pl.ds(0, size, stride=2), :], tmp[pl.ds(1, size, stride=2), :]], axis=1)
    pooled[...] = jnp.concatenate([v, sides(v)], axis=1)

    v = dot([window(pooled, 0, h_mid, half, dy).astype(bf16) for dy in range(3)], c_m1[...])
    middle[...] = jnp.concatenate([v, sides(v)], axis=1)
    clear(middle, 2, tile_rows // 2, half)

    v = dot([window(middle, 0, h_coarse, half, dy).astype(bf16) for dy in range(3)], c_m2[...])
    size = h_coarse * half
    tmp[pl.ds(0, size, stride=2), :] = v[:, :CH]
    tmp[pl.ds(1, size, stride=2), :] = v[:, CH:]
    v = tmp[: 2 * size, :]
    up[...] = jnp.concatenate([rolled(v, 1), v, rolled(v, -1)], axis=1).astype(bf16)
    clear(up, 1, tile_rows // 2, line)

    def dec_step(par):
        def skip3(t, p):
            return skip[t : t + h_dec, p * line : (p + 1) * line, :].reshape(h_dec * line, 4 * CH)

        if par == 0:
            windows = [skip3(2, 0), skip3(2, 1), skip3(3, 0)]
        else:
            windows = [skip3(2, 1), skip3(3, 0), skip3(3, 1)]
        windows += [window(up, 0, h_dec, line, d) for d in range(2)]
        v = dot(windows, c_d1[par])

        def compact(value):
            value = value.reshape(h_dec, 2, groups, 8, value.shape[1])
            turned = [pltpu.roll(value[:, :, g].reshape(h_dec * 2, 8, -1), 4, 1) for g in range(groups)]
            parts = [
                jnp.where(upper, turned[g], turned[g + 1]).reshape(h_dec, 2, 8, -1)
                for g in range(groups - 1)
            ]
            return jnp.concatenate(parts, axis=2).reshape(h_dec, 2 * own, -1)

        both = jnp.concatenate([compact(v), compact(sides(v))], axis=2)
        dec[:, par * 2 * own : (par + 1) * 2 * own, :] = both.astype(bf16)

    dec_step(0)
    dec_step(1)

    @pl.when(at_top)
    def _():
        dec[0, : 2 * own] = jnp.zeros((2 * own, 4 * CH), bf16)

    @pl.when(at_bottom)
    def _():
        dec[h_dec - 1, 2 * own :] = jnp.zeros((2 * own, 4 * CH), bf16)

    n = tile_rows // 2

    def last_step(py):
        windows = [
            dec[d // 2 : d // 2 + n, d % 2 * 2 * own : (d % 2 + 1) * 2 * own, :].reshape(n * 2 * own, 4 * CH)
            for d in range(py, py + 3)
        ]
        v = dot(windows, c_d2[...])
        z = jnp.dot(v.astype(bf16), c_out[...], preferred_element_type=f32)
        z = z.reshape(n, 2 * own, 2 * CH)
        for px in range(2):
            for b in range(2):
                piece = z[:, b * own : (b + 1) * own, px * CH : (px + 1) * CH]
                last[:, pl.ds(py * 4 * own + 2 * px + b, own, stride=4), :] = piece

    last_step(0)
    last_step(1)
    out_ref[...] = last[...].reshape(n * 8 * own, CH)[:, :FIELDS].astype(bf16)


FIRST_CHUNKS, SKIP_CHUNKS, DEC_CHUNKS = 2, 2, 2


def unet_scratch(tile_rows, tile_cols):
    line = 2 * pairs_of(tile_cols)
    half = line // 2
    h_pool = (tile_rows + 12) // 2
    return [
        pltpu.VMEM(((tile_rows + 2 * HALO) * line, 2 * CH), bf16),
        pltpu.VMEM(((tile_rows + 14) * line, 4 * CH), bf16),
        pltpu.VMEM((h_pool, 2 * line, 4 * CH), bf16),
        pltpu.VMEM((h_pool * line, CH), f32),
        pltpu.VMEM((h_pool * half, 4 * CH), f32),
        pltpu.VMEM(((h_pool - 2) * half, 4 * CH), f32),
        pltpu.VMEM(((h_pool - 4) * line, 3 * CH), bf16),
        pltpu.VMEM((tile_rows // 2 + 1, 2 * tile_cols, 4 * CH), bf16),
        pltpu.VMEM((tile_rows // 2, 4 * tile_cols, CH), f32),
    ]


def weight_scratch():
    square = pltpu.VMEM((12 * CH, 2 * CH), bf16)
    return [
        pltpu.VMEM((12 * FIELDS, 2 * CH), bf16), square, square, square,
        pltpu.VMEM((2, 18 * CH, 2 * CH), bf16), square, pltpu.VMEM((2 * CH, 2 * CH), bf16),
    ]


def whole_kernel(tile_rows, tile_cols, *refs):
    ins, w_hbm, final, scratch = refs[:4], refs[4:11], refs[11], refs[12:]
    w_vmem, w_sem, mats = scratch[:7], scratch[7], scratch[8:15]
    pad, own, unet_refs = scratch[15], scratch[16:36], scratch[36:]

    def weights_start():
        for i in range(7):
            pltpu.make_async_copy(w_hbm[i], w_vmem[i], w_sem.at[i]).start()

    def weights_ready():
        for i in range(7):
            pltpu.make_async_copy(w_hbm[i], w_vmem[i], w_sem.at[i]).wait()
        prepare(*w_vmem, *mats)

    regrid_body(tile_rows, tile_cols, weights_start, weights_ready, *ins, pad, *own)
    row = lax.axis_index("row")
    unet_body(
        tile_rows, tile_cols, row == 0, row == lax.axis_size("row") - 1, pad, mats, final, *unet_refs
    )


def regrid_body(
    tile_rows, tile_cols, weights_start, weights_ready, src_in, req_in, sten_in, wgt_in, pad,
    src_ref, req_ref, sten_ref, wgt_ref, load, asks, reqs, src_t, mix, outbox, inbox, acc, slot_rows, weight_rows,
    req_send, req_recv, box_send, box_recv, halo_send, halo_recv,
):
    row, me = lax.axis_index("row"), lax.axis_index("col")
    n_row, n = lax.axis_size("row"), lax.axis_size("col")
    cap = req_ref.shape[1]
    cells = src_ref.shape[0]
    spots = tile_rows * tile_cols
    has_up, has_down = row > 0, row < n_row - 1
    wide = HALO // 2
    blocks = tile_cols // HALO
    edge = HALO * wide
    inner = tile_rows * wide

    loads = [
        pltpu.make_async_copy(outer, held, load.at[i])
        for i, (outer, held) in enumerate(
            [(req_in, req_ref), (src_in, src_ref), (sten_in, sten_ref), (wgt_in, wgt_ref)]
        )
    ]
    for copy in loads:
        copy.start()

    barrier = pltpu.get_barrier_semaphore()

    def greet(r, c):
        pl.semaphore_signal(
            barrier, inc=1, device_id=(r, lax.rem(c + n, n)), device_id_type=MESH
        )

    @pl.loop(1, n)
    def _(step):
        greet(row, me + step)

    @pl.when(has_up)
    def _():
        for d in (-1, 0, 1):
            greet(row - 1, me + d)

    @pl.when(has_down)
    def _():
        for d in (-1, 0, 1):
            greet(row + 1, me + d)

    weights_start()
    loads[0].wait()
    parts = cap // CH
    for j in range(n):
        for part in range(parts):
            asks[j, part : part + 1, :] = req_ref[j : j + 1, part * CH : (part + 1) * CH]

    rows_beside = jnp.minimum(row, 1) + jnp.minimum(n_row - 1 - row, 1)
    pl.semaphore_wait(barrier, n - 1 + 3 * rows_beside)

    def ask(step, sender):
        dest = lax.rem(me + step, n)
        return pltpu.make_async_remote_copy(
            src_ref=asks.at[dest],
            dst_ref=reqs.at[sender],
            send_sem=req_send.at[step],
            recv_sem=req_recv.at[sender],
            device_id=(row, dest),
            device_id_type=MESH,
        )

    @pl.loop(1, n)
    def _(step):
        ask(step, me).start()

    reqs[me] = asks[me]
    loads[1].wait()
    src_t[...] = src_ref[...].astype(f32).T.astype(bf16)

    loads[2].wait()
    loads[3].wait()
    taps = sten_ref.shape[0] // tile_rows
    lane = lax.broadcasted_iota(jnp.int32, (tile_cols, spots), 1)
    cell = lax.broadcasted_iota(jnp.int32, (tile_cols, spots), 0)
    column = lane // (spots // 2) + lane % wide * 2 + lane // inner % blocks * HALO
    turn = jnp.where(cell == column, 1.0, 0.0).astype(bf16)
    held = tile_rows * taps
    mine = lax.broadcasted_iota(jnp.int32, (held, spots), 0) // taps == (
        lax.broadcasted_iota(jnp.int32, (held, spots), 1) // wide % tile_rows
    )

    def in_order(values):
        spread = jnp.dot(values.astype(bf16), turn, preferred_element_type=f32)
        spread = jnp.where(mine, spread, 0.0).reshape(held // 8, 8, spots)
        total = jnp.sum(spread, axis=0)
        return total[:taps] + total[taps:]

    slots = sten_ref[...]
    slot_rows[...] = in_order((slots // 256).astype(f32)) * 256.0 + in_order((slots % 256).astype(f32))
    weight_rows[...] = in_order(wgt_ref[...])
    tile, piece = 16, 256

    def ladder(width):
        return lax.broadcasted_iota(jnp.int32, (tile, width), 0).astype(f32).astype(bf16)

    def spread(values):
        return jnp.broadcast_to(values, (tile, values.shape[1])).astype(bf16)

    lanes = min(512, spots)
    zero, one = jnp.zeros((), bf16), jnp.ones((), bf16)

    def mix_block(j):
        for left_lane in range(0, spots, lanes):
            here = slice(left_lane, left_lane + lanes)
            ids = ladder(lanes)
            weights = [spread(weight_rows[k : k + 1, here]) for k in range(taps)]
            for start in range(0, cap, piece):
                base = (j * cap + start).astype(f32)
                near = [spread(slot_rows[k : k + 1, here] - base) for k in range(taps)]
                for g in range(0, min(piece, cap), tile):
                    step_ids = ids + jnp.asarray(g, bf16)
                    total = None
                    for k in range(taps):
                        part = jnp.where(step_ids == near[k], weights[k], zero)
                        total = part if total is None else total + part
                    mix[j, start + g : start + g + tile, here] = total

    @pl.loop(0, n // 2)
    def _(j):
        mix_block(j)

    def picked(dest):
        asked = jnp.concatenate(
            [reqs[dest, part : part + 1, :] for part in range(parts)], axis=1
        ).astype(f32)
        ids = ladder(cap)
        rows = []
        for start in range(0, cells, piece):
            near = spread(asked - float(start))
            for g in range(0, piece, tile):
                rows.append(jnp.where(ids + jnp.asarray(g, bf16) == near, one, zero))
        hot = jnp.concatenate(rows, axis=0)
        return jnp.dot(src_t[...], hot, preferred_element_type=f32).astype(bf16)

    def post(step, sender):
        return pltpu.make_async_remote_copy(
            src_ref=outbox.at[step],
            dst_ref=inbox.at[sender],
            send_sem=box_send.at[step],
            recv_sem=box_recv.at[sender],
            device_id=(row, lax.rem(me + step, n)),
            device_id_type=MESH,
        )

    @pl.loop(1, n)
    def _(step):
        dest = lax.rem(me + step, n)
        ask(step, dest).wait_recv()
        outbox[step] = picked(dest)
        post(step, me).start()

    inbox[me] = picked(me)

    @pl.loop(n // 2, n)
    def _(j):
        mix_block(j)

    acc[...] = jnp.dot(inbox[me], mix[me], preferred_element_type=f32)
    weights_ready()

    @pl.loop(1, n)
    def _(step):
        sender = lax.rem(me - step + n, n)
        post(step, sender).wait_recv()
        acc[...] += jnp.dot(inbox[sender], mix[sender], preferred_element_type=f32)

    for par in range(2):
        turned = acc[:, par * spots // 2 : (par + 1) * spots // 2].T.astype(bf16)
        lanes_here = slice(par * CH, (par + 1) * CH)
        for xb in range(blocks):
            pad[xb + 1, edge : edge + inner, lanes_here] = turned[xb * inner : (xb + 1) * inner]

    @pl.when(jnp.logical_not(has_up))
    def _():
        pad[:, :edge] = jnp.zeros((blocks + 2, edge, 2 * CH), bf16)

    @pl.when(jnp.logical_not(has_down))
    def _():
        pad[:, edge + inner :] = jnp.zeros((blocks + 2, edge, 2 * CH), bf16)

    mid = slice(edge, edge + inner)
    first, last = slice(edge, 2 * edge), slice(inner, inner + edge)
    low, high = slice(0, edge), slice(edge + inner, 2 * edge + inner)
    every = slice(1, blocks + 1)
    left, right = slice(1, 2), slice(blocks, blocks + 1)
    before, after = slice(0, 1), slice(blocks + 1, blocks + 2)
    moves = [
        (0, 1, (right, mid), (before, mid)),
        (0, -1, (left, mid), (after, mid)),
        (1, 0, (every, last), (every, low)),
        (1, 1, (right, last), (before, low)),
        (1, -1, (left, last), (after, low)),
        (-1, 0, (every, first), (every, high)),
        (-1, 1, (right, first), (before, high)),
        (-1, -1, (left, first), (after, high)),
    ]

    def shift(i):
        dr, dc, src, dst = moves[i]
        return pltpu.make_async_remote_copy(
            src_ref=pad.at[src[0], src[1]],
            dst_ref=pad.at[dst[0], dst[1]],
            send_sem=halo_send.at[i],
            recv_sem=halo_recv.at[i],
            device_id=(row + dr, lax.rem(me + dc + n, n)),
            device_id_type=MESH,
        )

    @pl.when(has_down)
    def _():
        for i in (2, 3, 4):
            shift(i).start()

    @pl.when(has_up)
    def _():
        for i in (5, 6, 7):
            shift(i).start()

    for i in (0, 1):
        shift(i).start()

    @pl.loop(1, n)
    def _(step):
        ask(step, me).wait_send()
        post(step, me).wait_send()

    for i in (0, 1):
        shift(i).wait()

    @pl.when(has_up)
    def _():
        for i in (2, 3, 4):
            shift(i).wait_recv()

    @pl.when(has_down)
    def _():
        for i in (5, 6, 7):
            shift(i).wait_recv()

    @pl.when(has_down)
    def _():
        for i in (2, 3, 4):
            shift(i).wait_send()

    @pl.when(has_up)
    def _():
        for i in (5, 6, 7):
            shift(i).wait_send()


def forward(source, wanted, stencil, weight, weights, tile_rows, tile_cols):
    n, cap = wanted.shape
    cells, columns = source.shape
    spots = tile_rows * tile_cols
    blocks = tile_cols // HALO
    rows = tile_rows + 2 * HALO
    taps = stencil.shape[0] // tile_rows
    dma = pltpu.SemaphoreType.DMA
    return pl.pallas_call(
        functools.partial(whole_kernel, tile_rows, tile_cols),
        out_shape=jax.ShapeDtypeStruct((2 * spots, FIELDS), bf16),
        in_specs=[pl.BlockSpec(memory_space=pltpu.HBM)] * 11,
        out_specs=pl.BlockSpec(memory_space=pltpu.VMEM),
        scratch_shapes=[pltpu.VMEM(w.shape, bf16) for w in weights]
        + [dma((7,))]
        + weight_scratch()
        + [
            pltpu.VMEM((blocks + 2, rows * HALO // 2, 2 * columns), bf16),
            pltpu.VMEM(source.shape, bf16),
            pltpu.VMEM(wanted.shape, jnp.int32),
            pltpu.VMEM(stencil.shape, jnp.int32),
            pltpu.VMEM(weight.shape, f32),
            dma((4,)),
            pltpu.VMEM((n, cap // CH, CH), jnp.int32),
            pltpu.VMEM((n, cap // CH, CH), jnp.int32),
            pltpu.VMEM((columns, cells), bf16),
            pltpu.VMEM((n, cap, spots), bf16),
            pltpu.VMEM((n, columns, cap), bf16),
            pltpu.VMEM((n, columns, cap), bf16),
            pltpu.VMEM((columns, spots), f32),
            pltpu.VMEM((taps, spots), f32),
            pltpu.VMEM((taps, spots), f32),
            dma((n,)), dma((n,)), dma((n,)), dma((n,)), dma((8,)), dma((8,)),
        ]
        + unet_scratch(tile_rows, tile_cols),
        compiler_params=pltpu.CompilerParams(
            collective_id=0, has_side_effects=True, vmem_limit_bytes=60 * 1024 * 1024
        ),
        cost_estimate=pl.CostEstimate(
            flops=10**9, bytes_accessed=2 * 10**6, transcendentals=0
        ),
    )(source, wanted, stencil, weight, *weights)


def body(source_tiles, requests, stencil, regrid_weight, *weights):
    tile_rows, tile_cols, taps = stencil.shape
    cells, columns = source_tiles.shape[2:]
    result = forward(
        source_tiles.reshape(cells, columns),
        requests.reshape(requests.shape[2:]),
        stencil.transpose(0, 2, 1).reshape(tile_rows * taps, tile_cols),
        regrid_weight.transpose(0, 2, 1).reshape(tile_rows * taps, tile_cols),
        (*weights[:-1], weights[-1].T),
        tile_rows,
        tile_cols,
    )
    return result.reshape(tile_rows, tile_cols, 2, FIELDS)


def solution(mesh):
    placed = (P("row", "col", None, None),) * 2 + (P("row", "col", None),) * 2 + (P(),) * 7
    return jax.shard_map(
        body, mesh=mesh, in_specs=placed, out_specs=P("row", "col", None, None), check_vma=False
    )
```

```python
import functools

import jax
import jax.numpy as jnp
from jax import lax
from jax.experimental import pallas as pl
from jax.experimental.pallas import tpu as pltpu
from jax.sharding import PartitionSpec as P

FIELDS = 64
CH = 128
HALO = 8
f32, bf16 = jnp.float32, jnp.bfloat16
MESH = pl.DeviceIdType.MESH


def silu(a):
    return a * (0.5 + 0.5 * jnp.tanh(0.5 * a))


def pair_weight(out, base, w, dy):
    zero = jnp.zeros((CH, CH), bf16)
    rows = [
        (w[dy, 1], w[dy, 0]), (w[dy, 2], w[dy, 1]), (w[dy, 0], zero), (zero, w[dy, 2])
    ]
    for i, (even, odd) in enumerate(rows):
        place = slice(base + i * CH, base + (i + 1) * CH)
        out[place, :CH] = even
        out[place, CH:] = odd


def prepare(w_in, w_enc, w_m1, w_m2, w_d1, w_d2, w_out, c_in, c_enc, c_m1, c_m2, c_d1, c_d2, c_out):
    quad = 4 * FIELDS
    none = jnp.zeros((FIELDS, CH), bf16)
    for dy in range(3):
        for j in range(4):
            place = slice(dy * quad + j * FIELDS, dy * quad + (j + 1) * FIELDS)
            c_in[place, :CH] = w_in[dy, j] if j < 3 else none
            c_in[place, CH:] = w_in[dy, j - 1] if j > 0 else none
        base = dy * 4 * CH
        pair_weight(c_enc, base, w_enc, dy)
        pair_weight(c_m1, base, w_m1, dy)
        pair_weight(c_m2, base, w_m2, dy)
        pair_weight(c_d2, base, w_d2, dy)
        for par in range(2):
            pair_weight(c_d1.at[par], base, w_d1.at[:, :, CH:], dy)
    zero = jnp.zeros((CH, CH), bf16)
    for par in range(2):
        groups = ((0, 1), (2,)) if par == 0 else ((0,), (1, 2))
        for g, dys in enumerate(groups):
            taps = [sum(w_d1[dy, dx, :CH].astype(f32) for dy in dys) for dx in range(3)]
            base = 12 * CH + g * 3 * CH
            rows = [
                (taps[0].astype(bf16), zero),
                ((taps[1] + taps[2]).astype(bf16), (taps[0] + taps[1]).astype(bf16)),
                (zero, taps[2].astype(bf16)),
            ]
            for i, (even, odd) in enumerate(rows):
                place = slice(base + i * CH, base + (i + 1) * CH)
                c_d1[par, place, :CH] = even
                c_d1[par, place, CH:] = odd
    last = w_out[...].astype(f32).T.astype(bf16)
    pad = jnp.zeros((CH, CH - FIELDS), bf16)
    full = jnp.concatenate([last.astype(f32), pad.astype(f32)], axis=1).astype(bf16)
    c_out[:CH, :CH] = full
    c_out[CH:, CH:] = full
    c_out[:CH, CH:] = zero
    c_out[CH:, :CH] = zero


def pairs_of(tile_cols):
    return tile_cols // 2 + HALO


def unet_body(tile_rows, tile_cols, at_top, at_bottom, pad, weights, dec, quad, first, skip, tmp, pooled, middle, up):
    c_in, c_enc, c_m1, c_m2, c_d1 = weights
    rows = tile_rows + 2 * HALO
    pairs = pairs_of(tile_cols)
    line = 2 * pairs
    half = line // 2
    h_first, h_skip = tile_rows + 14, tile_rows + 12
    h_pool = h_skip // 2
    h_mid, h_coarse = h_pool - 2, h_pool - 4
    h_dec = (tile_rows + 2) // 2
    own = tile_cols // 2
    low = lax.broadcasted_iota(jnp.int32, (1, 1, CH), 2) < FIELDS
    upper = lax.broadcasted_iota(jnp.int32, (1, 8, 1), 1) < 4
    groups = pairs // 8

    def rolled(value, by):
        return pltpu.roll(value, by % value.shape[0], 0)

    def line_up(start, count):
        columns = []
        for par in range(2):
            lanes = slice(par * CH, (par + 1) * CH)
            parts = []
            for g in range(groups):
                place = pl.ds(start * 4, count * 4)
                a = pad[2 * g, place, lanes].astype(f32).reshape(count // 2, 8, CH)
                b = pad[2 * g + 1, place, lanes].astype(f32).reshape(count // 2, 8, CH)
                turned_a, turned_b = pltpu.roll(a, 4, 1), pltpu.roll(b, 4, 1)
                both = jnp.stack(
                    [jnp.where(upper, a, turned_b), jnp.where(upper, turned_a, b)], axis=1
                )
                parts.append(both.reshape(count, 8, CH))
            columns.append(jnp.concatenate(parts, axis=1).reshape(count * pairs, CH))
        even, odd = columns
        even_t, odd_t = pltpu.roll(even, FIELDS, 1), pltpu.roll(odd, FIELDS, 1)
        before, before_t = rolled(odd, 1), rolled(odd_t, 1)
        after, after_t = rolled(even, -1), rolled(even_t, -1)
        lo = low.reshape(1, CH)
        one = [jnp.where(lo, before, even_t), jnp.where(lo, odd, after_t)]
        two = [jnp.where(lo, before_t, even), jnp.where(lo, odd_t, after)]
        both = [
            jnp.concatenate(v, axis=1).reshape(count, pairs, 2 * CH) for v in (one, two)
        ]
        value = jnp.concatenate(both, axis=1).reshape(count * line, 2 * CH).astype(bf16)
        quad[pl.ds(start * line, count * line), :] = value

    step = 16
    @pl.loop(0, rows // step)
    def _(i):
        line_up(pl.multiple_of(i * step, step), step)

    def dot(windows, weight):
        return silu(
            jnp.dot(jnp.concatenate(windows, axis=1), weight, preferred_element_type=f32)
        )

    def sides(value):
        return jnp.concatenate([rolled(value[:, CH:], 1), rolled(value[:, :CH], -1)], axis=1)

    def window(ref, start, count, width, dy):
        return ref[pl.ds(pl.multiple_of((start + dy) * width, 8), count * width), :]

    def clear(ref, depth, inner, width):
        @pl.when(at_top)
        def _():
            ref[: depth * width] = jnp.zeros((depth * width, ref.shape[1]), ref.dtype)

        @pl.when(at_bottom)
        def _():
            ref[(depth + inner) * width :] = jnp.zeros((depth * width, ref.shape[1]), ref.dtype)

    def chunks(total, count, fn):
        if total == count:
            fn(0)
        else:
            @pl.loop(0, total // count)
            def _(i):
                fn(i * count)

    count = h_first // FIRST_CHUNKS

    def first_step(start):
        v = dot([window(quad, start, count, line, dy) for dy in range(3)], c_in[...])
        v = jnp.concatenate([v, sides(v)], axis=1).astype(bf16)
        first[pl.ds(pl.multiple_of(start * line, 16), count * line), :] = v

    chunks(h_first, count, first_step)
    clear(first, 7, tile_rows, line)

    count_s = h_skip // SKIP_CHUNKS

    def skip_step(start):
        v = dot([window(first, start, count_s, line, dy) for dy in range(3)], c_enc[...])
        both = jnp.concatenate([v, sides(v)], axis=1).astype(bf16)
        skip[pl.ds(start // 2, count_s // 2)] = both.reshape(count_s // 2, 2 * line, 4 * CH)
        v = v.reshape(count_s // 2, 2 * line, 2 * CH)
        v = (v[:, :line] + v[:, line:]).reshape(count_s // 2 * line, 2 * CH)
        place = pl.ds(pl.multiple_of(start * line // 2, 8), count_s // 2 * line)
        tmp[place, :] = (v[:, :CH] + v[:, CH:]) * 0.25

    chunks(h_skip, count_s, skip_step)

    @pl.when(at_top)
    def _():
        skip[:3] = jnp.zeros((3, 2 * line, 4 * CH), bf16)

    @pl.when(at_bottom)
    def _():
        skip[h_pool - 3 :] = jnp.zeros((3, 2 * line, 4 * CH), bf16)

    @pl.when(at_top)
    def _():
        tmp[: 3 * line] = jnp.zeros((3 * line, CH), f32)

    @pl.when(at_bottom)
    def _():
        tmp[(h_pool - 3) * line :] = jnp.zeros((3 * line, CH), f32)

    size = h_pool * half
    v = jnp.concatenate([tmp[pl.ds(0, size, stride=2), :], tmp[pl.ds(1, size, stride=2), :]], axis=1)
    pooled[...] = jnp.concatenate([v, sides(v)], axis=1)

    v = dot([window(pooled, 0, h_mid, half, dy).astype(bf16) for dy in range(3)], c_m1[...])
    middle[...] = jnp.concatenate([v, sides(v)], axis=1)
    clear(middle, 2, tile_rows // 2, half)

    v = dot([window(middle, 0, h_coarse, half, dy).astype(bf16) for dy in range(3)], c_m2[...])
    size = h_coarse * half
    tmp[pl.ds(0, size, stride=2), :] = v[:, :CH]
    tmp[pl.ds(1, size, stride=2), :] = v[:, CH:]
    v = tmp[: 2 * size, :]
    up[...] = jnp.concatenate([rolled(v, 1), v, rolled(v, -1)], axis=1).astype(bf16)
    clear(up, 1, tile_rows // 2, line)

    def dec_step(par):
        def skip3(t, p):
            return skip[t : t + h_dec, p * line : (p + 1) * line, :].reshape(h_dec * line, 4 * CH)

        if par == 0:
            windows = [skip3(2, 0), skip3(2, 1), skip3(3, 0)]
        else:
            windows = [skip3(2, 1), skip3(3, 0), skip3(3, 1)]
        windows += [window(up, 0, h_dec, line, d) for d in range(2)]
        v = dot(windows, c_d1[par])

        def compact(value):
            value = value.reshape(h_dec, 2, groups, 8, value.shape[1])
            turned = [pltpu.roll(value[:, :, g].reshape(h_dec * 2, 8, -1), 4, 1) for g in range(groups)]
            parts = [
                jnp.where(upper, turned[g], turned[g + 1]).reshape(h_dec, 2, 8, -1)
                for g in range(groups - 1)
            ]
            return jnp.concatenate(parts, axis=2).reshape(h_dec, 2 * own, -1)

        both = jnp.concatenate([compact(v), compact(sides(v))], axis=2)
        both = both.astype(bf16)
        for i in range(h_dec):
            dec[2 * i + par] = both[i]

    dec_step(0)
    dec_step(1)

    @pl.when(at_top)
    def _():
        dec[0] = jnp.zeros((2 * own, 4 * CH), bf16)

    @pl.when(at_bottom)
    def _():
        dec[2 * h_dec - 1] = jnp.zeros((2 * own, 4 * CH), bf16)


def tail_body(tile_rows, own, dec, c_d2, c_out, last, put):
    n = tile_rows // TAIL_CHUNKS
    for i in range(TAIL_CHUNKS):
        windows = [
            dec[i * n + dy : (i + 1) * n + dy].reshape(n * 2 * own, 4 * CH) for dy in range(3)
        ]
        v = silu(
            jnp.dot(jnp.concatenate(windows, axis=1), c_d2[...], preferred_element_type=f32)
        )
        z = jnp.dot(v.astype(bf16), c_out[...], preferred_element_type=f32)
        z = z.reshape(n, 2 * own, 2 * CH)
        for px in range(2):
            for b in range(2):
                piece = z[:, b * own : (b + 1) * own, px * CH : (px + 1) * CH]
                last[pl.ds(i * n * own * 4 + 2 * px + b, n * own, stride=4), :] = piece.reshape(n * own, CH)
        put(i * n * own * 4, n * own * 4)


TAIL_CHUNKS = 2
FIRST_CHUNKS, SKIP_CHUNKS = 2, 2


def unet_scratch(tile_rows, tile_cols):
    line = 2 * pairs_of(tile_cols)
    half = line // 2
    h_pool = (tile_rows + 12) // 2
    return [
        pltpu.VMEM(((tile_rows + 2 * HALO) * line, 2 * CH), bf16),
        pltpu.VMEM(((tile_rows + 14) * line, 4 * CH), bf16),
        pltpu.VMEM((h_pool, 2 * line, 4 * CH), bf16),
        pltpu.VMEM((h_pool * line, CH), f32),
        pltpu.VMEM((h_pool * half, 4 * CH), f32),
        pltpu.VMEM(((h_pool - 2) * half, 4 * CH), f32),
        pltpu.VMEM(((h_pool - 4) * line, 3 * CH), bf16),
    ]


def weight_scratch():
    square = pltpu.VMEM((12 * CH, 2 * CH), bf16)
    return [
        pltpu.VMEM((12 * FIELDS, 2 * CH), bf16), square, square, square,
        pltpu.VMEM((2, 18 * CH, 2 * CH), bf16),
    ]


def whole_kernel(tile_rows, tile_cols, *refs):
    ins, w_hbm, outs, scratch = refs[:4], refs[4:11], refs[11:14], refs[14:]
    w_vmem, w_sem, mats = scratch[:7], scratch[7], scratch[8:13]
    pad, own, unet_refs = scratch[13], scratch[14:34], scratch[34:]
    dec, c_d2, c_out = outs

    def weights_start():
        for i in range(7):
            pltpu.make_async_copy(w_hbm[i], w_vmem[i], w_sem.at[i]).start()

    def weights_ready():
        for i in range(7):
            pltpu.make_async_copy(w_hbm[i], w_vmem[i], w_sem.at[i]).wait()
        prepare(*w_vmem, *mats, c_d2, c_out)

    regrid_body(tile_rows, tile_cols, weights_start, weights_ready, *ins, pad, *own)
    row = lax.axis_index("row")
    unet_body(
        tile_rows, tile_cols, row == 0, row == lax.axis_size("row") - 1, pad, mats, dec, *unet_refs
    )


def tail_kernel(tile_rows, own, dec, c_d2, c_out, out_ref, last, staged, sem):
    copies = []

    def put(start, count):
        place = slice(start, start + count)
        staged[place, :] = last[place, :FIELDS].astype(bf16)
        copy = pltpu.make_async_copy(staged.at[place], out_ref.at[place], sem.at[len(copies)])
        copy.start()
        copies.append(copy)

    tail_body(tile_rows, own, dec, c_d2, c_out, last, put)
    for copy in copies:
        copy.wait()


def tail(dec, c_d2, c_out):
    tile_rows, tile_cols = dec.shape[0] - 2, dec.shape[1]
    cells = 2 * tile_rows * tile_cols
    return pl.pallas_call(
        functools.partial(tail_kernel, tile_rows, tile_cols // 2),
        out_shape=jax.ShapeDtypeStruct((cells, FIELDS), bf16),
        in_specs=[pl.BlockSpec(memory_space=pltpu.VMEM)] * 3,
        out_specs=pl.BlockSpec(memory_space=pltpu.HBM),
        scratch_shapes=[
            pltpu.VMEM((cells, CH), f32),
            pltpu.VMEM((cells, FIELDS), bf16),
            pltpu.SemaphoreType.DMA((TAIL_CHUNKS,)),
        ],
        compiler_params=pltpu.CompilerParams(vmem_limit_bytes=16 * 1024 * 1024),
        cost_estimate=pl.CostEstimate(
            flops=10**9, bytes_accessed=2 * 10**6, transcendentals=0
        ),
    )(dec, c_d2, c_out)


def regrid_body(
    tile_rows, tile_cols, weights_start, weights_ready, src_in, req_in, sten_in, wgt_in, pad,
    src_ref, req_ref, sten_ref, wgt_ref, load, asks, reqs, src_t, mix, outbox, inbox, acc, slot_rows, weight_rows,
    req_send, req_recv, box_send, box_recv, halo_send, halo_recv,
):
    row, me = lax.axis_index("row"), lax.axis_index("col")
    n_row, n = lax.axis_size("row"), lax.axis_size("col")
    cap = req_ref.shape[1]
    cells = src_ref.shape[0]
    spots = tile_rows * tile_cols
    has_up, has_down = row > 0, row < n_row - 1
    wide = HALO // 2
    blocks = tile_cols // HALO
    edge = HALO * wide
    inner = tile_rows * wide

    loads = [
        pltpu.make_async_copy(outer, held, load.at[i])
        for i, (outer, held) in enumerate(
            [(req_in, req_ref), (src_in, src_ref), (sten_in, sten_ref), (wgt_in, wgt_ref)]
        )
    ]
    for copy in loads:
        copy.start()

    barrier = pltpu.get_barrier_semaphore()

    def greet(r, c):
        pl.semaphore_signal(
            barrier, inc=1, device_id=(r, lax.rem(c + n, n)), device_id_type=MESH
        )

    @pl.loop(1, n)
    def _(step):
        greet(row, me + step)

    @pl.when(has_up)
    def _():
        for d in (-1, 0, 1):
            greet(row - 1, me + d)

    @pl.when(has_down)
    def _():
        for d in (-1, 0, 1):
            greet(row + 1, me + d)

    weights_start()
    loads[0].wait()
    parts = cap // CH
    for j in range(n):
        for part in range(parts):
            asks[j, part : part + 1, :] = req_ref[j : j + 1, part * CH : (part + 1) * CH]

    rows_beside = jnp.minimum(row, 1) + jnp.minimum(n_row - 1 - row, 1)
    pl.semaphore_wait(barrier, n - 1 + 3 * rows_beside)

    def ask(step, sender):
        dest = lax.rem(me + step, n)
        return pltpu.make_async_remote_copy(
            src_ref=asks.at[dest],
            dst_ref=reqs.at[sender],
            send_sem=req_send.at[step],
            recv_sem=req_recv.at[sender],
            device_id=(row, dest),
            device_id_type=MESH,
        )

    @pl.loop(1, n)
    def _(step):
        ask(step, me).start()

    reqs[me] = asks[me]
    loads[1].wait()
    src_t[...] = src_ref[...].astype(f32).T.astype(bf16)

    loads[2].wait()
    loads[3].wait()
    taps = sten_ref.shape[0] // tile_rows
    lane = lax.broadcasted_iota(jnp.int32, (tile_cols, spots), 1)
    cell = lax.broadcasted_iota(jnp.int32, (tile_cols, spots), 0)
    column = lane // (spots // 2) + lane % wide * 2 + lane // inner % blocks * HALO
    turn = jnp.where(cell == column, 1.0, 0.0).astype(bf16)
    held = tile_rows * taps
    mine = lax.broadcasted_iota(jnp.int32, (held, spots), 0) // taps == (
        lax.broadcasted_iota(jnp.int32, (held, spots), 1) // wide % tile_rows
    )

    def in_order(values):
        spread = jnp.dot(values.astype(bf16), turn, preferred_element_type=f32)
        spread = jnp.where(mine, spread, 0.0).reshape(held // 8, 8, spots)
        total = jnp.sum(spread, axis=0)
        return total[:taps] + total[taps:]

    slots = sten_ref[...]
    slot_rows[...] = in_order((slots // 256).astype(f32)) * 256.0 + in_order((slots % 256).astype(f32))
    weight_rows[...] = in_order(wgt_ref[...])
    tile, piece = 16, 256

    def ladder(width):
        return lax.broadcasted_iota(jnp.int32, (tile, width), 0).astype(f32).astype(bf16)

    def spread(values):
        return jnp.broadcast_to(values, (tile, values.shape[1])).astype(bf16)

    lanes = min(512, spots)
    zero, one = jnp.zeros((), bf16), jnp.ones((), bf16)

    def mix_block(j):
        for left_lane in range(0, spots, lanes):
            here = slice(left_lane, left_lane + lanes)
            ids = ladder(lanes)
            weights = [spread(weight_rows[k : k + 1, here]) for k in range(taps)]
            for start in range(0, cap, piece):
                base = (j * cap + start).astype(f32)
                near = [spread(slot_rows[k : k + 1, here] - base) for k in range(taps)]
                for g in range(0, min(piece, cap), tile):
                    step_ids = ids + jnp.asarray(g, bf16)
                    total = None
                    for k in range(taps):
                        part = jnp.where(step_ids == near[k], weights[k], zero)
                        total = part if total is None else total + part
                    mix[j, start + g : start + g + tile, here] = total

    @pl.loop(0, n // 2)
    def _(j):
        mix_block(j)

    def picked(dest):
        asked = jnp.concatenate(
            [reqs[dest, part : part + 1, :] for part in range(parts)], axis=1
        ).astype(f32)
        ids = ladder(cap)
        rows = []
        for start in range(0, cells, piece):
            near = spread(asked - float(start))
            for g in range(0, piece, tile):
                rows.append(jnp.where(ids + jnp.asarray(g, bf16) == near, one, zero))
        hot = jnp.concatenate(rows, axis=0)
        return jnp.dot(src_t[...], hot, preferred_element_type=f32).astype(bf16)

    def post(step, sender):
        return pltpu.make_async_remote_copy(
            src_ref=outbox.at[step],
            dst_ref=inbox.at[sender],
            send_sem=box_send.at[step],
            recv_sem=box_recv.at[sender],
            device_id=(row, lax.rem(me + step, n)),
            device_id_type=MESH,
        )

    @pl.loop(1, n)
    def _(step):
        dest = lax.rem(me + step, n)
        ask(step, dest).wait_recv()
        outbox[step] = picked(dest)
        post(step, me).start()

    inbox[me] = picked(me)

    @pl.loop(n // 2, n)
    def _(j):
        mix_block(j)

    acc[...] = jnp.dot(inbox[me], mix[me], preferred_element_type=f32)
    weights_ready()

    @pl.loop(1, n)
    def _(step):
        sender = lax.rem(me - step + n, n)
        post(step, sender).wait_recv()
        acc[...] += jnp.dot(inbox[sender], mix[sender], preferred_element_type=f32)

    for par in range(2):
        turned = acc[:, par * spots // 2 : (par + 1) * spots // 2].T.astype(bf16)
        lanes_here = slice(par * CH, (par + 1) * CH)
        for xb in range(blocks):
            pad[xb + 1, edge : edge + inner, lanes_here] = turned[xb * inner : (xb + 1) * inner]

    @pl.when(jnp.logical_not(has_up))
    def _():
        pad[:, :edge] = jnp.zeros((blocks + 2, edge, 2 * CH), bf16)

    @pl.when(jnp.logical_not(has_down))
    def _():
        pad[:, edge + inner :] = jnp.zeros((blocks + 2, edge, 2 * CH), bf16)

    mid = slice(edge, edge + inner)
    first, last = slice(edge, 2 * edge), slice(inner, inner + edge)
    low, high = slice(0, edge), slice(edge + inner, 2 * edge + inner)
    every = slice(1, blocks + 1)
    left, right = slice(1, 2), slice(blocks, blocks + 1)
    before, after = slice(0, 1), slice(blocks + 1, blocks + 2)
    moves = [
        (0, 1, (right, mid), (before, mid)),
        (0, -1, (left, mid), (after, mid)),
        (1, 0, (every, last), (every, low)),
        (1, 1, (right, last), (before, low)),
        (1, -1, (left, last), (after, low)),
        (-1, 0, (every, first), (every, high)),
        (-1, 1, (right, first), (before, high)),
        (-1, -1, (left, first), (after, high)),
    ]

    def shift(i):
        dr, dc, src, dst = moves[i]
        return pltpu.make_async_remote_copy(
            src_ref=pad.at[src[0], src[1]],
            dst_ref=pad.at[dst[0], dst[1]],
            send_sem=halo_send.at[i],
            recv_sem=halo_recv.at[i],
            device_id=(row + dr, lax.rem(me + dc + n, n)),
            device_id_type=MESH,
        )

    @pl.when(has_down)
    def _():
        for i in (2, 3, 4):
            shift(i).start()

    @pl.when(has_up)
    def _():
        for i in (5, 6, 7):
            shift(i).start()

    for i in (0, 1):
        shift(i).start()

    @pl.loop(1, n)
    def _(step):
        ask(step, me).wait_send()
        post(step, me).wait_send()

    for i in (0, 1):
        shift(i).wait()

    @pl.when(has_up)
    def _():
        for i in (2, 3, 4):
            shift(i).wait_recv()

    @pl.when(has_down)
    def _():
        for i in (5, 6, 7):
            shift(i).wait_recv()

    @pl.when(has_down)
    def _():
        for i in (2, 3, 4):
            shift(i).wait_send()

    @pl.when(has_up)
    def _():
        for i in (5, 6, 7):
            shift(i).wait_send()


def forward(source, wanted, stencil, weight, weights, tile_rows, tile_cols):
    n, cap = wanted.shape
    cells, columns = source.shape
    spots = tile_rows * tile_cols
    blocks = tile_cols // HALO
    rows = tile_rows + 2 * HALO
    taps = stencil.shape[0] // tile_rows
    dma = pltpu.SemaphoreType.DMA
    return pl.pallas_call(
        functools.partial(whole_kernel, tile_rows, tile_cols),
        out_shape=[
            pltpu.VMEM(shape, bf16)
            for shape in ((tile_rows + 2, tile_cols, 4 * CH), (12 * CH, 2 * CH), (2 * CH, 2 * CH))
        ],
        in_specs=[pl.BlockSpec(memory_space=pltpu.HBM)] * 11,
        out_specs=[pl.BlockSpec(memory_space=pltpu.VMEM)] * 3,
        scratch_shapes=[pltpu.VMEM(w.shape, bf16) for w in weights]
        + [dma((7,))]
        + weight_scratch()
        + [
            pltpu.VMEM((blocks + 2, rows * HALO // 2, 2 * columns), bf16),
            pltpu.VMEM(source.shape, bf16),
            pltpu.VMEM(wanted.shape, jnp.int32),
            pltpu.VMEM(stencil.shape, jnp.int32),
            pltpu.VMEM(weight.shape, f32),
            dma((4,)),
            pltpu.VMEM((n, cap // CH, CH), jnp.int32),
            pltpu.VMEM((n, cap // CH, CH), jnp.int32),
            pltpu.VMEM((columns, cells), bf16),
            pltpu.VMEM((n, cap, spots), bf16),
            pltpu.VMEM((n, columns, cap), bf16),
            pltpu.VMEM((n, columns, cap), bf16),
            pltpu.VMEM((columns, spots), f32),
            pltpu.VMEM((taps, spots), f32),
            pltpu.VMEM((taps, spots), f32),
            dma((n,)), dma((n,)), dma((n,)), dma((n,)), dma((8,)), dma((8,)),
        ]
        + unet_scratch(tile_rows, tile_cols),
        compiler_params=pltpu.CompilerParams(
            collective_id=0, has_side_effects=True, vmem_limit_bytes=40 * 1024 * 1024
        ),
        cost_estimate=pl.CostEstimate(
            flops=10**9, bytes_accessed=2 * 10**6, transcendentals=0
        ),
    )(*[pltpu.with_memory_space_constraint(a, pltpu.HBM) for a in (source, wanted, stencil, weight, *weights)])


def body(source_tiles, requests, stencil, regrid_weight, *weights):
    tile_rows, tile_cols, taps = stencil.shape
    cells, columns = source_tiles.shape[2:]
    done = forward(
        source_tiles.reshape(cells, columns),
        requests.reshape(requests.shape[2:]),
        stencil.transpose(0, 2, 1).reshape(tile_rows * taps, tile_cols),
        regrid_weight.transpose(0, 2, 1).reshape(tile_rows * taps, tile_cols),
        (*weights[:-1], weights[-1].T),
        tile_rows,
        tile_cols,
    )
    return tail(*done).reshape(tile_rows, tile_cols, 2, FIELDS)


def solution(mesh):
    placed = (P("row", "col", None, None),) * 2 + (P("row", "col", None),) * 2 + (P(),) * 7
    return jax.shard_map(
        body, mesh=mesh, in_specs=placed, out_specs=P("row", "col", None, None), check_vma=False
    )
```

```python
import functools

import jax
import jax.numpy as jnp
from jax import lax
from jax.experimental import pallas as pl
from jax.experimental.pallas import tpu as pltpu
from jax.sharding import PartitionSpec as P

FIELDS = 64
CH = 128
HALO = 8
f32, bf16 = jnp.float32, jnp.bfloat16
MESH = pl.DeviceIdType.MESH


def silu(a):
    return a * (0.5 + 0.5 * jnp.tanh(0.5 * a))


def pair_weight(out, base, w, dy):
    zero = jnp.zeros((CH, CH), bf16)
    rows = [
        (w[dy, 1], w[dy, 0]), (w[dy, 2], w[dy, 1]), (w[dy, 0], zero), (zero, w[dy, 2])
    ]
    for i, (even, odd) in enumerate(rows):
        place = slice(base + i * CH, base + (i + 1) * CH)
        out[place, :CH] = even
        out[place, CH:] = odd


def prepare(w_in, w_enc, w_m1, w_m2, w_d1, w_d2, w_out, c_in, c_enc, c_m1, c_m2, c_d1, c_d2, c_out):
    quad = 4 * FIELDS
    none = jnp.zeros((FIELDS, CH), bf16)
    for dy in range(3):
        for j in range(4):
            place = slice(dy * quad + j * FIELDS, dy * quad + (j + 1) * FIELDS)
            c_in[place, :CH] = w_in[dy, j] if j < 3 else none
            c_in[place, CH:] = w_in[dy, j - 1] if j > 0 else none
        base = dy * 4 * CH
        pair_weight(c_enc, base, w_enc, dy)
        pair_weight(c_m1, base, w_m1, dy)
        pair_weight(c_m2, base, w_m2, dy)
        pair_weight(c_d2, base, w_d2, dy)
        for par in range(2):
            pair_weight(c_d1.at[par], base, w_d1.at[:, :, CH:], dy)
    zero = jnp.zeros((CH, CH), bf16)
    for par in range(2):
        groups = ((0, 1), (2,)) if par == 0 else ((0,), (1, 2))
        for g, dys in enumerate(groups):
            taps = [sum(w_d1[dy, dx, :CH].astype(f32) for dy in dys) for dx in range(3)]
            base = 12 * CH + g * 3 * CH
            rows = [
                (taps[0].astype(bf16), zero),
                ((taps[1] + taps[2]).astype(bf16), (taps[0] + taps[1]).astype(bf16)),
                (zero, taps[2].astype(bf16)),
            ]
            for i, (even, odd) in enumerate(rows):
                place = slice(base + i * CH, base + (i + 1) * CH)
                c_d1[par, place, :CH] = even
                c_d1[par, place, CH:] = odd
    last = w_out[...].astype(f32).T.astype(bf16)
    pad = jnp.zeros((CH, CH - FIELDS), bf16)
    full = jnp.concatenate([last.astype(f32), pad.astype(f32)], axis=1).astype(bf16)
    c_out[:CH, :CH] = full
    c_out[CH:, CH:] = full
    c_out[:CH, CH:] = zero
    c_out[CH:, :CH] = zero


def split(total, parts):
    size = -(-total // (2 * parts)) * 2
    return [(at, min(size, total - at)) for at in range(0, total, size)]


FIRST_CHUNKS, SKIP_CHUNKS = 2, 2


def pairs_of(tile_cols):
    return tile_cols // 2 + HALO


def unet_body(tile_rows, tile_cols, at_top, at_bottom, halo_here, pad, weights, dec, quad, first, skip, tmp, pooled, middle, up):
    c_in, c_enc, c_m1, c_m2, c_d1 = weights
    rows = tile_rows + 2 * HALO
    pairs = pairs_of(tile_cols)
    line = 2 * pairs
    half = line // 2
    h_first, h_skip = tile_rows + 14, tile_rows + 12
    h_pool = h_skip // 2
    h_mid, h_coarse = h_pool - 2, h_pool - 4
    h_dec = (tile_rows + 2) // 2
    own = tile_cols // 2
    top_scale = jnp.where(at_top, 0.0, 1.0).astype(f32)
    bottom_scale = jnp.where(at_bottom, 0.0, 1.0).astype(f32)
    low = lax.broadcasted_iota(jnp.int32, (1, CH), 1) < FIELDS
    upper = lax.broadcasted_iota(jnp.int32, (1, 8, 1), 1) < 4
    groups = pairs // 8

    def rolled(value, by):
        return pltpu.roll(value, by % value.shape[0], 0)

    def line_up(b):
        parts = []
        for g in range(groups):
            x, y = [
                pad[b, 2 * g + i].astype(f32).reshape(rows // 2, 8, CH) for i in range(2)
            ]
            turned_x, turned_y = pltpu.roll(x, 4, 1), pltpu.roll(y, 4, 1)
            both = jnp.stack(
                [jnp.where(upper, x, turned_y), jnp.where(upper, turned_x, y)], axis=1
            )
            parts.append(both.reshape(rows, 8, CH))
        value = jnp.concatenate(parts, axis=1).reshape(rows * pairs, CH)
        value = pltpu.roll(value, FIELDS, 1)
        value = jnp.concatenate(
            [
                jnp.where(low, rolled(value, 1), value),
                jnp.where(low, value, rolled(value, -1)),
            ],
            axis=1,
        )
        keep(quad, b, 0, value)

    def keep(ref, b, at, value):
        place = slice(at * pairs, at * pairs + value.shape[0])
        ref[b, 0, place] = value.astype(bf16)
        if at == 0:
            ref[b, 1, : value.shape[0] - pairs] = value[pairs:].astype(bf16)
        else:
            ref[b, 1, place.start - pairs : place.stop - pairs] = value.astype(bf16)

    def three(ref, b, at, count):
        start, size = at * pairs, count * pairs
        return [
            ref[b, 0, start : start + size],
            ref[b, 1, start : start + size],
            ref[b, 0, start + 2 * pairs : start + 2 * pairs + size],
        ]

    def inside(value, at, count, depth, total, width):
        above = max(0, min(depth, at + count) - at) * width
        below = max(0, at + count - max(at, total - depth)) * width
        parts = [value[:above] * top_scale] if above else []
        parts.append(value[above : value.shape[0] - below])
        if below:
            parts.append(value[value.shape[0] - below :] * bottom_scale)
        return jnp.concatenate(parts, axis=0)

    def dot(windows, weight):
        return silu(
            jnp.dot(jnp.concatenate(windows, axis=1), weight, preferred_element_type=f32)
        )

    def sides(value):
        return jnp.concatenate([rolled(value[:, CH:], 1), rolled(value[:, :CH], -1)], axis=1)

    def window(ref, start, count, width, dy):
        return ref[pl.ds(pl.multiple_of((start + dy) * width, 8), count * width), :]

    def encode(b):
        line_up(b)
        for at, count in split(h_first, FIRST_CHUNKS):
            v = dot(three(quad, b, at, count), c_in[...])
            v = inside(v, at, count, 7, h_first, pairs)
            keep(first, b, at, jnp.concatenate([v, sides(v)], axis=1))
        for at, count in split(h_skip, SKIP_CHUNKS):
            v = dot(three(first, b, at, count), c_enc[...])
            v = inside(v, at, count, 6, h_skip, pairs)
            half_rows = count // 2
            both = jnp.concatenate([v, sides(v)], axis=1).reshape(half_rows, 2, pairs, 4 * CH).astype(bf16)
            for par in range(2):
                place = par * line + b * pairs
                skip[at // 2 : at // 2 + half_rows, place : place + pairs, :] = both[:, par]
            v = v.reshape(half_rows, 2 * pairs, 2 * CH)
            v = v[:, :pairs] + v[:, pairs:]
            v = (v[:, :, :CH] + v[:, :, CH:]) * 0.25
            for t in range(half_rows):
                place = (at // 2 + t) * line + b * pairs
                tmp[place : place + pairs, :] = v[t]

    for b in range(2):
        halo_here(b)
        encode(b)

    size = h_pool * half
    v = jnp.concatenate([tmp[pl.ds(0, size, stride=2), :], tmp[pl.ds(1, size, stride=2), :]], axis=1)
    pooled[...] = jnp.concatenate([v, sides(v)], axis=1)

    v = dot([window(pooled, 0, h_mid, half, dy).astype(bf16) for dy in range(3)], c_m1[...])
    v = inside(v, 0, h_mid, 2, h_mid, half)
    middle[...] = jnp.concatenate([v, sides(v)], axis=1)

    v = dot([window(middle, 0, h_coarse, half, dy).astype(bf16) for dy in range(3)], c_m2[...])
    size = h_coarse * half
    tmp[pl.ds(0, size, stride=2), :] = v[:, :CH]
    tmp[pl.ds(1, size, stride=2), :] = v[:, CH:]
    v = inside(tmp[: 2 * size, :], 0, h_coarse, 1, h_coarse, line)
    up[...] = jnp.concatenate([rolled(v, 1), v, rolled(v, -1)], axis=1).astype(bf16)

    def dec_step(par):
        def skip3(t, p):
            return skip[t : t + h_dec, p * line : (p + 1) * line, :].reshape(h_dec * line, 4 * CH)

        if par == 0:
            windows = [skip3(2, 0), skip3(2, 1), skip3(3, 0)]
        else:
            windows = [skip3(2, 1), skip3(3, 0), skip3(3, 1)]
        windows += [window(up, 0, h_dec, line, d) for d in range(2)]
        v = dot(windows, c_d1[par])
        if par == 0:
            v = jnp.concatenate([v[:line] * top_scale, v[line:]], axis=0)
        else:
            v = jnp.concatenate([v[:-line], v[-line:] * bottom_scale], axis=0)

        def compact(value):
            value = value.reshape(h_dec, 2, groups, 8, value.shape[1])
            turned = [pltpu.roll(value[:, :, g].reshape(h_dec * 2, 8, -1), 4, 1) for g in range(groups)]
            parts = [
                jnp.where(upper, turned[g], turned[g + 1]).reshape(h_dec, 2, 8, -1)
                for g in range(groups - 1)
            ]
            return jnp.concatenate(parts, axis=2).reshape(h_dec, 2 * own, -1)

        both = jnp.concatenate([compact(v), compact(sides(v))], axis=2)
        both = both.astype(bf16)
        for i in range(h_dec):
            dec[2 * i + par] = both[i]

    dec_step(0)
    dec_step(1)


def tail_body(tile_rows, own, dec, c_d2, c_out, last, put):
    n = tile_rows // TAIL_CHUNKS
    for i in range(TAIL_CHUNKS):
        windows = [
            dec[i * n + dy : (i + 1) * n + dy].reshape(n * 2 * own, 4 * CH) for dy in range(3)
        ]
        v = silu(
            jnp.dot(jnp.concatenate(windows, axis=1), c_d2[...], preferred_element_type=f32)
        )
        z = jnp.dot(v.astype(bf16), c_out[...], preferred_element_type=f32)
        z = z.reshape(n, 2 * own, 2 * CH)
        for px in range(2):
            for b in range(2):
                piece = z[:, b * own : (b + 1) * own, px * CH : (px + 1) * CH]
                last[pl.ds(i * n * own * 4 + 2 * px + b, n * own, stride=4), :] = piece.reshape(n * own, CH)
        put(i * n * own * 4, n * own * 4)


TAIL_CHUNKS = 1


def unet_scratch(tile_rows, tile_cols):
    line = 2 * pairs_of(tile_cols)
    half = line // 2
    h_pool = (tile_rows + 12) // 2
    return [
        pltpu.VMEM((2, 2, (tile_rows + 2 * HALO) * half, 2 * CH), bf16),
        pltpu.VMEM((2, 2, (tile_rows + 14) * half, 4 * CH), bf16),
        pltpu.VMEM((h_pool, 2 * line, 4 * CH), bf16),
        pltpu.VMEM((h_pool * line, CH), f32),
        pltpu.VMEM((h_pool * half, 4 * CH), f32),
        pltpu.VMEM(((h_pool - 2) * half, 4 * CH), f32),
        pltpu.VMEM(((h_pool - 4) * line, 3 * CH), bf16),
    ]


def weight_scratch():
    square = pltpu.VMEM((12 * CH, 2 * CH), bf16)
    return [
        pltpu.VMEM((12 * FIELDS, 2 * CH), bf16), square, square, square,
        pltpu.VMEM((2, 18 * CH, 2 * CH), bf16),
    ]


def whole_kernel(tile_rows, tile_cols, *refs):
    ins, w_hbm, outs, scratch = refs[:4], refs[4:11], refs[11:14], refs[14:]
    w_vmem, w_sem, mats = scratch[:7], scratch[7], scratch[8:13]
    pad, own, unet_refs = scratch[13], scratch[14:34], scratch[34:]
    dec, c_d2, c_out = outs

    def weights_start():
        for i in range(7):
            pltpu.make_async_copy(w_hbm[i], w_vmem[i], w_sem.at[i]).start()

    def weights_ready():
        for i in range(7):
            pltpu.make_async_copy(w_hbm[i], w_vmem[i], w_sem.at[i]).wait()
        prepare(*w_vmem, *mats, c_d2, c_out)

    halo_here, sent = regrid_body(
        tile_rows, tile_cols, weights_start, weights_ready, *ins, pad, *own
    )
    row = lax.axis_index("row")
    unet_body(
        tile_rows, tile_cols, row == 0, row == lax.axis_size("row") - 1,
        halo_here, pad, mats, dec, *unet_refs,
    )
    sent()


def tail_kernel(tile_rows, own, dec, c_d2, c_out, out_ref, last, staged, sem):
    copies = []

    def put(start, count):
        place = slice(start, start + count)
        staged[place, :] = last[place, :FIELDS].astype(bf16)
        copy = pltpu.make_async_copy(staged.at[place], out_ref.at[place], sem.at[len(copies)])
        copy.start()
        copies.append(copy)

    tail_body(tile_rows, own, dec, c_d2, c_out, last, put)
    for copy in copies:
        copy.wait()


def tail(dec, c_d2, c_out):
    tile_rows, tile_cols = dec.shape[0] - 2, dec.shape[1]
    cells = 2 * tile_rows * tile_cols
    return pl.pallas_call(
        functools.partial(tail_kernel, tile_rows, tile_cols // 2),
        out_shape=jax.ShapeDtypeStruct((cells, FIELDS), bf16),
        in_specs=[pl.BlockSpec(memory_space=pltpu.VMEM)] * 3,
        out_specs=pl.BlockSpec(memory_space=pltpu.HBM),
        scratch_shapes=[
            pltpu.VMEM((cells, CH), f32),
            pltpu.VMEM((cells, FIELDS), bf16),
            pltpu.SemaphoreType.DMA((TAIL_CHUNKS,)),
        ],
        compiler_params=pltpu.CompilerParams(vmem_limit_bytes=16 * 1024 * 1024),
        cost_estimate=pl.CostEstimate(
            flops=10**9, bytes_accessed=2 * 10**6, transcendentals=0
        ),
    )(dec, c_d2, c_out)


EARLY = 0


def regrid_body(
    tile_rows, tile_cols, weights_start, weights_ready, src_in, req_in, sten_in, wgt_in, pad,
    src_ref, req_ref, sten_ref, wgt_ref, load, asks, reqs, src_t, mix, outbox, inbox, acc, slot_rows, weight_rows,
    req_send, req_recv, box_send, box_recv, halo_send, halo_recv,
):
    row, me = lax.axis_index("row"), lax.axis_index("col")
    n_row, n = lax.axis_size("row"), lax.axis_size("col")
    cap = req_ref.shape[1]
    cells = src_ref.shape[0]
    spots = tile_rows * tile_cols
    has_up, has_down = row > 0, row < n_row - 1
    wide = HALO // 2
    blocks = tile_cols // HALO
    edge = HALO * wide
    inner = tile_rows * wide

    loads = [
        pltpu.make_async_copy(outer, held, load.at[i])
        for i, (outer, held) in enumerate(
            [(req_in, req_ref), (src_in, src_ref), (sten_in, sten_ref), (wgt_in, wgt_ref)]
        )
    ]
    for copy in loads:
        copy.start()

    barrier = pltpu.get_barrier_semaphore()

    def greet(r, c):
        pl.semaphore_signal(
            barrier, inc=1, device_id=(r, lax.rem(c + n, n)), device_id_type=MESH
        )

    @pl.loop(1, n)
    def _(step):
        greet(row, me + step)

    @pl.when(has_up)
    def _():
        for d in (-1, 0, 1):
            greet(row - 1, me + d)

    @pl.when(has_down)
    def _():
        for d in (-1, 0, 1):
            greet(row + 1, me + d)

    weights_start()
    loads[0].wait()
    parts = cap // CH
    for j in range(n):
        for part in range(parts):
            asks[j, part : part + 1, :] = req_ref[j : j + 1, part * CH : (part + 1) * CH]

    rows_beside = jnp.minimum(row, 1) + jnp.minimum(n_row - 1 - row, 1)
    pl.semaphore_wait(barrier, n - 1 + 3 * rows_beside)

    def partner(step, sign):
        chip = lax.rem(me // 2 + sign * (step // 2) + n, n // 2)
        return chip * 2 + lax.rem(me + step, 2)

    def ask(step, sender):
        dest = partner(step, 1)
        return pltpu.make_async_remote_copy(
            src_ref=asks.at[dest],
            dst_ref=reqs.at[sender],
            send_sem=req_send.at[step],
            recv_sem=req_recv.at[sender],
            device_id=(row, dest),
            device_id_type=MESH,
        )

    @pl.loop(1, n)
    def _(i):
        ask(n - i, me).start()

    reqs[me] = asks[me]
    loads[1].wait()
    src_t[...] = src_ref[...].astype(f32).T.astype(bf16)

    loads[2].wait()
    loads[3].wait()
    taps = sten_ref.shape[0] // tile_rows
    lane = lax.broadcasted_iota(jnp.int32, (tile_cols, spots), 1)
    cell = lax.broadcasted_iota(jnp.int32, (tile_cols, spots), 0)
    column = lane // (spots // 2) + lane % wide * 2 + lane // inner % blocks * HALO
    turn = jnp.where(cell == column, 1.0, 0.0).astype(bf16)
    held = tile_rows * taps
    mine = lax.broadcasted_iota(jnp.int32, (held, spots), 0) // taps == (
        lax.broadcasted_iota(jnp.int32, (held, spots), 1) // wide % tile_rows
    )

    def in_order(values):
        spread = jnp.dot(values.astype(bf16), turn, preferred_element_type=f32)
        spread = jnp.where(mine, spread, 0.0).reshape(held // 8, 8, spots)
        total = jnp.sum(spread, axis=0)
        return total[:taps] + total[taps:]

    slots = sten_ref[...]
    slot_rows[...] = in_order((slots // 256).astype(f32)) * 256.0 + in_order((slots % 256).astype(f32))
    weight_rows[...] = in_order(wgt_ref[...])
    tile, piece = 16, 256

    def ladder(width):
        return lax.broadcasted_iota(jnp.int32, (tile, width), 0).astype(f32).astype(bf16)

    def spread(values):
        return jnp.broadcast_to(values, (tile, values.shape[1])).astype(bf16)

    lanes = min(512, spots)
    zero, one = jnp.zeros((), bf16), jnp.ones((), bf16)

    def mix_block(j):
        for left_lane in range(0, spots, lanes):
            here = slice(left_lane, left_lane + lanes)
            ids = ladder(lanes)
            weights = [spread(weight_rows[k : k + 1, here]) for k in range(taps)]
            for start in range(0, cap, piece):
                base = (j * cap + start).astype(f32)
                near = [spread(slot_rows[k : k + 1, here] - base) for k in range(taps)]
                for g in range(0, min(piece, cap), tile):
                    step_ids = ids + jnp.asarray(g, bf16)
                    total = None
                    for k in range(taps):
                        part = jnp.where(step_ids == near[k], weights[k], zero)
                        total = part if total is None else total + part
                    mix[j, start + g : start + g + tile, here] = total

    @pl.loop(0, EARLY)
    def _(j):
        mix_block(j)

    def picked(dest):
        asked = jnp.concatenate(
            [reqs[dest, part : part + 1, :] for part in range(parts)], axis=1
        ).astype(f32)
        ids = ladder(cap)
        rows = []
        for start in range(0, cells, piece):
            near = spread(asked - float(start))
            for g in range(0, piece, tile):
                rows.append(jnp.where(ids + jnp.asarray(g, bf16) == near, one, zero))
        hot = jnp.concatenate(rows, axis=0)
        return jnp.dot(src_t[...], hot, preferred_element_type=f32).astype(bf16)

    def post(step, sender, b):
        part = slice(b * FIELDS, (b + 1) * FIELDS)
        return pltpu.make_async_remote_copy(
            src_ref=outbox.at[step, part],
            dst_ref=inbox.at[sender, part],
            send_sem=box_send.at[b, step],
            recv_sem=box_recv.at[b, sender],
            device_id=(row, partner(step, 1)),
            device_id_type=MESH,
        )

    @pl.loop(1, n)
    def _(i):
        step = n - i
        dest = partner(step, 1)
        ask(step, dest).wait_recv()
        outbox[step] = picked(dest)
        post(step, me, 0).start()

    @pl.loop(1, n)
    def _(i):
        post(n - i, me, 1).start()

    inbox[me] = picked(me)

    @pl.loop(EARLY, n)
    def _(j):
        mix_block(j)

    def gather(b):
        part = slice(b * FIELDS, (b + 1) * FIELDS)
        acc[...] = jnp.dot(inbox[me, part], mix[me], preferred_element_type=f32)

        @pl.loop(1, n)
        def _(i):
            step = n - i
            sender = partner(step, -1)
            post(step, sender, b).wait_recv()
            acc[...] += jnp.dot(inbox[sender, part], mix[sender], preferred_element_type=f32)

        turned = jnp.concatenate([acc[:, : spots // 2], acc[:, spots // 2 :]], axis=0).T.astype(bf16)
        for xb in range(blocks):
            pad[b, xb + 1, edge : edge + inner] = turned[xb * inner : (xb + 1) * inner]

        @pl.when(jnp.logical_not(has_up))
        def _():
            pad[b, :, :edge] = jnp.zeros((blocks + 2, edge, CH), bf16)

        @pl.when(jnp.logical_not(has_down))
        def _():
            pad[b, :, edge + inner :] = jnp.zeros((blocks + 2, edge, CH), bf16)

    mid = slice(edge, edge + inner)
    first, last = slice(edge, 2 * edge), slice(inner, inner + edge)
    low, high = slice(0, edge), slice(edge + inner, 2 * edge + inner)
    every = slice(1, blocks + 1)
    left, right = slice(1, 2), slice(blocks, blocks + 1)
    before, after = slice(0, 1), slice(blocks + 1, blocks + 2)
    moves = [
        (0, 1, (right, mid), (before, mid)),
        (0, -1, (left, mid), (after, mid)),
        (1, 0, (every, last), (every, low)),
        (1, 1, (right, last), (before, low)),
        (1, -1, (left, last), (after, low)),
        (-1, 0, (every, first), (every, high)),
        (-1, 1, (right, first), (before, high)),
        (-1, -1, (left, first), (after, high)),
    ]

    def shift(i, b):
        dr, dc, src, dst = moves[i]
        return pltpu.make_async_remote_copy(
            src_ref=pad.at[b, src[0], src[1]],
            dst_ref=pad.at[b, dst[0], dst[1]],
            send_sem=halo_send.at[b, i],
            recv_sem=halo_recv.at[b, i],
            device_id=(row + dr, lax.rem(me + dc + n, n)),
            device_id_type=MESH,
        )

    def halo_start(b):
        @pl.when(has_down)
        def _():
            for i in (2, 3, 4):
                shift(i, b).start()

        @pl.when(has_up)
        def _():
            for i in (5, 6, 7):
                shift(i, b).start()

        for i in (0, 1):
            shift(i, b).start()

    def halo_here(b):
        for i in (0, 1):
            shift(i, b).wait_recv()

        @pl.when(has_up)
        def _():
            for i in (2, 3, 4):
                shift(i, b).wait_recv()

        @pl.when(has_down)
        def _():
            for i in (5, 6, 7):
                shift(i, b).wait_recv()

    def sent():
        @pl.loop(1, n)
        def _(step):
            ask(step, me).wait_send()
            for b in range(2):
                post(step, me, b).wait_send()

        for b in range(2):
            for i in (0, 1):
                shift(i, b).wait_send()

        @pl.when(has_down)
        def _():
            for b in range(2):
                for i in (2, 3, 4):
                    shift(i, b).wait_send()

        @pl.when(has_up)
        def _():
            for b in range(2):
                for i in (5, 6, 7):
                    shift(i, b).wait_send()

    gather(0)
    halo_start(0)
    weights_ready()
    gather(1)
    halo_start(1)
    return halo_here, sent


def forward(source, wanted, stencil, weight, weights, tile_rows, tile_cols):
    n, cap = wanted.shape
    cells, columns = source.shape
    spots = tile_rows * tile_cols
    blocks = tile_cols // HALO
    rows = tile_rows + 2 * HALO
    taps = stencil.shape[0] // tile_rows
    dma = pltpu.SemaphoreType.DMA
    return pl.pallas_call(
        functools.partial(whole_kernel, tile_rows, tile_cols),
        out_shape=[
            pltpu.VMEM(shape, bf16)
            for shape in ((tile_rows + 2, tile_cols, 4 * CH), (12 * CH, 2 * CH), (2 * CH, 2 * CH))
        ],
        in_specs=[pl.BlockSpec(memory_space=pltpu.HBM)] * 11,
        out_specs=[pl.BlockSpec(memory_space=pltpu.VMEM)] * 3,
        scratch_shapes=[pltpu.VMEM(w.shape, bf16) for w in weights]
        + [dma((7,))]
        + weight_scratch()
        + [
            pltpu.VMEM((2, blocks + 2, rows * HALO // 2, columns), bf16),
            pltpu.VMEM(source.shape, bf16),
            pltpu.VMEM(wanted.shape, jnp.int32),
            pltpu.VMEM(stencil.shape, jnp.int32),
            pltpu.VMEM(weight.shape, f32),
            dma((4,)),
            pltpu.VMEM((n, cap // CH, CH), jnp.int32),
            pltpu.VMEM((n, cap // CH, CH), jnp.int32),
            pltpu.VMEM((columns, cells), bf16),
            pltpu.VMEM((n, cap, spots), bf16),
            pltpu.VMEM((n, columns, cap), bf16),
            pltpu.VMEM((n, columns, cap), bf16),
            pltpu.VMEM((FIELDS, spots), f32),
            pltpu.VMEM((taps, spots), f32),
            pltpu.VMEM((taps, spots), f32),
            dma((n,)), dma((n,)), dma((2, n)), dma((2, n)), dma((2, 8)), dma((2, 8)),
        ]
        + unet_scratch(tile_rows, tile_cols),
        compiler_params=pltpu.CompilerParams(
            collective_id=0, has_side_effects=True, vmem_limit_bytes=40 * 1024 * 1024
        ),
        cost_estimate=pl.CostEstimate(
            flops=10**9, bytes_accessed=2 * 10**6, transcendentals=0
        ),
    )(*[pltpu.with_memory_space_constraint(a, pltpu.HBM) for a in (source, wanted, stencil, weight, *weights)])


def body(source_tiles, requests, stencil, regrid_weight, *weights):
    tile_rows, tile_cols, taps = stencil.shape
    cells, columns = source_tiles.shape[2:]
    done = forward(
        source_tiles.reshape(cells, columns),
        requests.reshape(requests.shape[2:]),
        stencil.transpose(0, 2, 1).reshape(tile_rows * taps, tile_cols),
        regrid_weight.transpose(0, 2, 1).reshape(tile_rows * taps, tile_cols),
        (*weights[:-1], weights[-1].T),
        tile_rows,
        tile_cols,
    )
    return tail(*done).reshape(tile_rows, tile_cols, 2, FIELDS)


def solution(mesh):
    placed = (P("row", "col", None, None),) * 2 + (P("row", "col", None),) * 2 + (P(),) * 7
    return jax.shard_map(
        body, mesh=mesh, in_specs=placed, out_specs=P("row", "col", None, None), check_vma=False
    )
```

```python
import functools

import jax
import jax.numpy as jnp
from jax import lax
from jax.experimental import pallas as pl
from jax.experimental.pallas import tpu as pltpu
from jax.sharding import PartitionSpec as P

FIELDS = 64
CH = 128
HALO = 8
f32, bf16 = jnp.float32, jnp.bfloat16
MESH = pl.DeviceIdType.MESH


def silu(a):
    return a * (0.5 + 0.5 * jnp.tanh(0.5 * a))


def pair_weight(out, base, w, dy):
    zero = jnp.zeros((CH, CH), bf16)
    rows = [
        (w[dy, 1], w[dy, 0]), (w[dy, 2], w[dy, 1]), (w[dy, 0], zero), (zero, w[dy, 2])
    ]
    for i, (even, odd) in enumerate(rows):
        place = slice(base + i * CH, base + (i + 1) * CH)
        out[place, :CH] = even
        out[place, CH:] = odd


def prepare(w_in, w_enc, w_m1, w_m2, w_d1, w_d2, w_out, c_in, c_enc, c_m1, c_m2, c_d1, c_d2, c_out):
    quad = 4 * FIELDS
    none = jnp.zeros((FIELDS, CH), bf16)
    for dy in range(3):
        for j in range(4):
            place = slice(dy * quad + j * FIELDS, dy * quad + (j + 1) * FIELDS)
            c_in[place, :CH] = w_in[dy, j] if j < 3 else none
            c_in[place, CH:] = w_in[dy, j - 1] if j > 0 else none
        base = dy * 4 * CH
        pair_weight(c_enc, base, w_enc, dy)
        pair_weight(c_m1, base, w_m1, dy)
        pair_weight(c_m2, base, w_m2, dy)
        pair_weight(c_d2, base, w_d2, dy)
        for par in range(2):
            pair_weight(c_d1.at[par], base, w_d1.at[:, :, CH:], dy)
    zero = jnp.zeros((CH, CH), bf16)
    for par in range(2):
        groups = ((0, 1), (2,)) if par == 0 else ((0,), (1, 2))
        for g, dys in enumerate(groups):
            taps = [sum(w_d1[dy, dx, :CH].astype(f32) for dy in dys) for dx in range(3)]
            base = 12 * CH + g * 3 * CH
            rows = [
                (taps[0].astype(bf16), zero),
                ((taps[1] + taps[2]).astype(bf16), (taps[0] + taps[1]).astype(bf16)),
                (zero, taps[2].astype(bf16)),
            ]
            for i, (even, odd) in enumerate(rows):
                place = slice(base + i * CH, base + (i + 1) * CH)
                c_d1[par, place, :CH] = even
                c_d1[par, place, CH:] = odd
    last = w_out[...].astype(f32).T.astype(bf16)
    pad = jnp.zeros((CH, CH - FIELDS), bf16)
    full = jnp.concatenate([last.astype(f32), pad.astype(f32)], axis=1).astype(bf16)
    c_out[:CH, :CH] = full
    c_out[CH:, CH:] = full
    c_out[:CH, CH:] = zero
    c_out[CH:, :CH] = zero


def split(total, parts):
    size = -(-total // (2 * parts)) * 2
    return [(at, min(size, total - at)) for at in range(0, total, size)]


FIRST_CHUNKS, SKIP_CHUNKS = 2, 2


def pairs_of(tile_cols):
    return tile_cols // 2 + HALO


def unet_body(tile_rows, tile_cols, at_top, at_bottom, halo_here, pad, weights, dec, quad, first, skip, tmp, pooled, middle, up, part):
    c_in, c_enc, c_m1, c_m2, c_d1 = weights
    rows = tile_rows + 2 * HALO
    pairs = pairs_of(tile_cols)
    line = 2 * pairs
    half = line // 2
    h_first, h_skip = tile_rows + 14, tile_rows + 12
    h_pool = h_skip // 2
    h_mid, h_coarse = h_pool - 2, h_pool - 4
    h_dec = (tile_rows + 2) // 2
    own = tile_cols // 2
    top_scale = jnp.where(at_top, 0.0, 1.0).astype(f32)
    bottom_scale = jnp.where(at_bottom, 0.0, 1.0).astype(f32)
    low = lax.broadcasted_iota(jnp.int32, (1, CH), 1) < FIELDS
    upper = lax.broadcasted_iota(jnp.int32, (1, 8, 1), 1) < 4
    groups = pairs // 8

    def rolled(value, by):
        return pltpu.roll(value, by % value.shape[0], 0)

    def line_up(b):
        parts = []
        for g in range(groups):
            x, y = [
                pad[b, 2 * g + i].astype(f32).reshape(rows // 2, 8, CH) for i in range(2)
            ]
            turned_x, turned_y = pltpu.roll(x, 4, 1), pltpu.roll(y, 4, 1)
            both = jnp.stack(
                [jnp.where(upper, x, turned_y), jnp.where(upper, turned_x, y)], axis=1
            )
            parts.append(both.reshape(rows, 8, CH))
        value = jnp.concatenate(parts, axis=1).reshape(rows * pairs, CH)
        value = pltpu.roll(value, FIELDS, 1)
        value = jnp.concatenate(
            [
                jnp.where(low, rolled(value, 1), value),
                jnp.where(low, value, rolled(value, -1)),
            ],
            axis=1,
        )
        keep(quad, b, 0, value)

    def keep(ref, b, at, value):
        place = slice(at * pairs, at * pairs + value.shape[0])
        ref[b, 0, place] = value.astype(bf16)
        if at == 0:
            ref[b, 1, : value.shape[0] - pairs] = value[pairs:].astype(bf16)
        else:
            ref[b, 1, place.start - pairs : place.stop - pairs] = value.astype(bf16)

    def three(ref, b, at, count):
        start, size = at * pairs, count * pairs
        return [
            ref[b, 0, start : start + size],
            ref[b, 1, start : start + size],
            ref[b, 0, start + 2 * pairs : start + 2 * pairs + size],
        ]

    def inside(value, at, count, depth, total, width):
        above = max(0, min(depth, at + count) - at) * width
        below = max(0, at + count - max(at, total - depth)) * width
        parts = [value[:above] * top_scale] if above else []
        parts.append(value[above : value.shape[0] - below])
        if below:
            parts.append(value[value.shape[0] - below :] * bottom_scale)
        return jnp.concatenate(parts, axis=0)

    def dot(windows, weight):
        return silu(
            jnp.dot(jnp.concatenate(windows, axis=1), weight, preferred_element_type=f32)
        )

    def sides(value):
        return jnp.concatenate([rolled(value[:, CH:], 1), rolled(value[:, :CH], -1)], axis=1)

    def window(ref, start, count, width, dy):
        return ref[pl.ds(pl.multiple_of((start + dy) * width, 8), count * width), :]

    def encode(b):
        line_up(b)
        for at, count in split(h_first, FIRST_CHUNKS):
            v = dot(three(quad, b, at, count), c_in[...])
            v = inside(v, at, count, 7, h_first, pairs)
            keep(first, b, at, jnp.concatenate([v, sides(v)], axis=1))
        for at, count in split(h_skip, SKIP_CHUNKS):
            v = dot(three(first, b, at, count), c_enc[...])
            v = inside(v, at, count, 6, h_skip, pairs)
            half_rows = count // 2
            both = jnp.concatenate([v, sides(v)], axis=1).reshape(half_rows, 2, pairs, 4 * CH)
            for par in range(2):
                piece = both[:, par].reshape(half_rows * pairs, 4 * CH)
                place = at // 2 * pairs
                skip[b, 0, par, place : place + half_rows * pairs] = piece.astype(bf16)
                if at == 0:
                    piece = piece[pairs:]
                else:
                    place -= pairs
                skip[b, 1, par, place : place + piece.shape[0]] = piece.astype(bf16)
            v = v.reshape(half_rows, 2 * pairs, 2 * CH)
            v = v[:, :pairs] + v[:, pairs:]
            v = (v[:, :, :CH] + v[:, :, CH:]) * 0.25
            for t in range(half_rows):
                place = (at // 2 + t) * line + b * pairs
                tmp[place : place + pairs, :] = v[t]
        for par in range(2):
            size = h_dec * pairs
            windows = [
                skip[b, d // 2, d % 2, 2 * pairs : 2 * pairs + size] for d in range(par, par + 3)
            ]
            part[b, par] = jnp.dot(
                jnp.concatenate(windows, axis=1), c_d1[par, : 12 * CH], preferred_element_type=f32
            )

    for b in range(2):
        halo_here(b)
        encode(b)

    size = h_pool * half
    v = jnp.concatenate([tmp[pl.ds(0, size, stride=2), :], tmp[pl.ds(1, size, stride=2), :]], axis=1)
    pooled[...] = jnp.concatenate([v, sides(v)], axis=1)

    v = dot([window(pooled, 0, h_mid, half, dy).astype(bf16) for dy in range(3)], c_m1[...])
    v = inside(v, 0, h_mid, 2, h_mid, half)
    middle[...] = jnp.concatenate([v, sides(v)], axis=1)

    v = dot([window(middle, 0, h_coarse, half, dy).astype(bf16) for dy in range(3)], c_m2[...])
    size = h_coarse * half
    tmp[pl.ds(0, size, stride=2), :] = v[:, :CH]
    tmp[pl.ds(1, size, stride=2), :] = v[:, CH:]
    v = inside(tmp[: 2 * size, :], 0, h_coarse, 1, h_coarse, line)
    v = jnp.concatenate([rolled(v, 1), v, rolled(v, -1)], axis=1).reshape(h_coarse, line, 3 * CH)
    for b in range(2):
        piece = v[:, b * pairs : (b + 1) * pairs].reshape(h_coarse * pairs, 3 * CH)
        up[b] = jnp.concatenate([piece[:-pairs], piece[pairs:]], axis=1).astype(bf16)

    def compact(value):
        value = value.reshape(h_dec, groups, 8, value.shape[1])
        turned = [pltpu.roll(value[:, g], 4, 1) for g in range(groups)]
        parts = [jnp.where(upper, turned[g], turned[g + 1]) for g in range(groups - 1)]
        return jnp.concatenate(parts, axis=1)

    for b in range(2):
        for par in range(2):
            v = part[b, par] + jnp.dot(up[b], c_d1[par, 12 * CH :], preferred_element_type=f32)
            v = silu(v)
            if par == 0:
                v = jnp.concatenate([v[:pairs] * top_scale, v[pairs:]], axis=0)
            else:
                v = jnp.concatenate([v[:-pairs], v[-pairs:] * bottom_scale], axis=0)
            both = jnp.concatenate([compact(v), compact(sides(v))], axis=2).astype(bf16)
            for i in range(h_dec):
                dec[2 * i + par, b * own : (b + 1) * own] = both[i]


def tail_body(tile_rows, own, dec, c_d2, c_out, last, put):
    n = tile_rows // TAIL_CHUNKS
    for i in range(TAIL_CHUNKS):
        windows = [
            dec[i * n + dy : (i + 1) * n + dy].reshape(n * 2 * own, 4 * CH) for dy in range(3)
        ]
        v = silu(
            jnp.dot(jnp.concatenate(windows, axis=1), c_d2[...], preferred_element_type=f32)
        )
        z = jnp.dot(v.astype(bf16), c_out[...], preferred_element_type=f32)
        z = z.reshape(n, 2 * own, 2 * CH)
        for px in range(2):
            for b in range(2):
                piece = z[:, b * own : (b + 1) * own, px * CH : (px + 1) * CH]
                last[pl.ds(i * n * own * 4 + 2 * px + b, n * own, stride=4), :] = piece.reshape(n * own, CH)
        put(i * n * own * 4, n * own * 4)


TAIL_CHUNKS = 1


def unet_scratch(tile_rows, tile_cols):
    line = 2 * pairs_of(tile_cols)
    half = line // 2
    h_pool = (tile_rows + 12) // 2
    return [
        pltpu.VMEM((2, 2, (tile_rows + 2 * HALO) * half, 2 * CH), bf16),
        pltpu.VMEM((2, 2, (tile_rows + 14) * half, 4 * CH), bf16),
        pltpu.VMEM((2, 2, 2, h_pool * half, 4 * CH), bf16),
        pltpu.VMEM((h_pool * line, CH), f32),
        pltpu.VMEM((h_pool * half, 4 * CH), f32),
        pltpu.VMEM(((h_pool - 2) * half, 4 * CH), f32),
        pltpu.VMEM((2, (h_pool - 5) * half, 6 * CH), bf16),
        pltpu.VMEM((2, 2, (h_pool - 5) * half, 2 * CH), f32),
    ]


def weight_scratch():
    square = pltpu.VMEM((12 * CH, 2 * CH), bf16)
    return [
        pltpu.VMEM((12 * FIELDS, 2 * CH), bf16), square, square, square,
        pltpu.VMEM((2, 18 * CH, 2 * CH), bf16),
    ]


def whole_kernel(tile_rows, tile_cols, *refs):
    ins, w_hbm, outs, scratch = refs[:4], refs[4:11], refs[11:14], refs[14:]
    w_vmem, w_sem, mats = scratch[:7], scratch[7], scratch[8:13]
    pad, own, unet_refs = scratch[13], scratch[14:34], scratch[34:]
    dec, c_d2, c_out = outs

    def weights_start():
        for i in range(7):
            pltpu.make_async_copy(w_hbm[i], w_vmem[i], w_sem.at[i]).start()

    def weights_ready():
        for i in range(7):
            pltpu.make_async_copy(w_hbm[i], w_vmem[i], w_sem.at[i]).wait()
        prepare(*w_vmem, *mats, c_d2, c_out)

    halo_here, sent = regrid_body(
        tile_rows, tile_cols, weights_start, weights_ready, *ins, pad, *own
    )
    row = lax.axis_index("row")
    unet_body(
        tile_rows, tile_cols, row == 0, row == lax.axis_size("row") - 1,
        halo_here, pad, mats, dec, *unet_refs,
    )
    sent()


def tail_kernel(tile_rows, own, dec, c_d2, c_out, out_ref, last, staged, sem):
    copies = []

    def put(start, count):
        place = slice(start, start + count)
        staged[place, :] = last[place, :FIELDS].astype(bf16)
        copy = pltpu.make_async_copy(staged.at[place], out_ref.at[place], sem.at[len(copies)])
        copy.start()
        copies.append(copy)

    tail_body(tile_rows, own, dec, c_d2, c_out, last, put)
    for copy in copies:
        copy.wait()


def tail(dec, c_d2, c_out):
    tile_rows, tile_cols = dec.shape[0] - 2, dec.shape[1]
    cells = 2 * tile_rows * tile_cols
    return pl.pallas_call(
        functools.partial(tail_kernel, tile_rows, tile_cols // 2),
        out_shape=jax.ShapeDtypeStruct((cells, FIELDS), bf16),
        in_specs=[pl.BlockSpec(memory_space=pltpu.VMEM)] * 3,
        out_specs=pl.BlockSpec(memory_space=pltpu.HBM),
        scratch_shapes=[
            pltpu.VMEM((cells, CH), f32),
            pltpu.VMEM((cells, FIELDS), bf16),
            pltpu.SemaphoreType.DMA((TAIL_CHUNKS,)),
        ],
        compiler_params=pltpu.CompilerParams(vmem_limit_bytes=16 * 1024 * 1024),
        cost_estimate=pl.CostEstimate(
            flops=10**9, bytes_accessed=2 * 10**6, transcendentals=0
        ),
    )(dec, c_d2, c_out)


EARLY = 0


def regrid_body(
    tile_rows, tile_cols, weights_start, weights_ready, src_in, req_in, sten_in, wgt_in, pad,
    src_ref, req_ref, sten_ref, wgt_ref, load, asks, reqs, src_t, mix, outbox, inbox, acc, slot_rows, weight_rows,
    req_send, req_recv, box_send, box_recv, halo_send, halo_recv,
):
    row, me = lax.axis_index("row"), lax.axis_index("col")
    n_row, n = lax.axis_size("row"), lax.axis_size("col")
    cap = req_ref.shape[1]
    cells = src_ref.shape[0]
    spots = tile_rows * tile_cols
    has_up, has_down = row > 0, row < n_row - 1
    wide = HALO // 2
    blocks = tile_cols // HALO
    edge = HALO * wide
    inner = tile_rows * wide

    loads = [
        pltpu.make_async_copy(outer, held, load.at[i])
        for i, (outer, held) in enumerate(
            [(req_in, req_ref), (src_in, src_ref), (sten_in, sten_ref), (wgt_in, wgt_ref)]
        )
    ]
    for copy in loads:
        copy.start()

    barrier = pltpu.get_barrier_semaphore()

    def greet(r, c):
        pl.semaphore_signal(
            barrier, inc=1, device_id=(r, lax.rem(c + n, n)), device_id_type=MESH
        )

    @pl.loop(1, n)
    def _(step):
        greet(row, me + step)

    @pl.when(has_up)
    def _():
        for d in (-1, 0, 1):
            greet(row - 1, me + d)

    @pl.when(has_down)
    def _():
        for d in (-1, 0, 1):
            greet(row + 1, me + d)

    weights_start()
    loads[0].wait()
    parts = cap // CH
    for j in range(n):
        for part in range(parts):
            asks[j, part : part + 1, :] = req_ref[j : j + 1, part * CH : (part + 1) * CH]

    rows_beside = jnp.minimum(row, 1) + jnp.minimum(n_row - 1 - row, 1)
    pl.semaphore_wait(barrier, n - 1 + 3 * rows_beside)

    def partner(step, sign):
        chip = lax.rem(me // 2 + sign * (step // 2) + n, n // 2)
        return chip * 2 + lax.rem(me + step, 2)

    def ask(step, sender):
        dest = partner(step, 1)
        return pltpu.make_async_remote_copy(
            src_ref=asks.at[dest],
            dst_ref=reqs.at[sender],
            send_sem=req_send.at[step],
            recv_sem=req_recv.at[sender],
            device_id=(row, dest),
            device_id_type=MESH,
        )

    @pl.loop(1, n)
    def _(i):
        ask(n - i, me).start()

    reqs[me] = asks[me]
    loads[1].wait()
    src_t[...] = src_ref[...].astype(f32).T.astype(bf16)

    loads[2].wait()
    loads[3].wait()
    taps = sten_ref.shape[0] // tile_rows
    lane = lax.broadcasted_iota(jnp.int32, (tile_cols, spots), 1)
    cell = lax.broadcasted_iota(jnp.int32, (tile_cols, spots), 0)
    column = lane // (spots // 2) + lane % wide * 2 + lane // inner % blocks * HALO
    turn = jnp.where(cell == column, 1.0, 0.0).astype(bf16)
    held = tile_rows * taps
    mine = lax.broadcasted_iota(jnp.int32, (held, spots), 0) // taps == (
        lax.broadcasted_iota(jnp.int32, (held, spots), 1) // wide % tile_rows
    )

    def in_order(values):
        spread = jnp.dot(values.astype(bf16), turn, preferred_element_type=f32)
        spread = jnp.where(mine, spread, 0.0).reshape(held // 8, 8, spots)
        total = jnp.sum(spread, axis=0)
        return total[:taps] + total[taps:]

    slots = sten_ref[...]
    slot_rows[...] = in_order((slots // 256).astype(f32)) * 256.0 + in_order((slots % 256).astype(f32))
    weight_rows[...] = in_order(wgt_ref[...])
    tile, piece = 16, 256

    def ladder(width):
        return lax.broadcasted_iota(jnp.int32, (tile, width), 0).astype(f32).astype(bf16)

    def spread(values):
        return jnp.broadcast_to(values, (tile, values.shape[1])).astype(bf16)

    lanes = min(512, spots)
    zero, one = jnp.zeros((), bf16), jnp.ones((), bf16)

    def mix_block(j):
        for left_lane in range(0, spots, lanes):
            here = slice(left_lane, left_lane + lanes)
            ids = ladder(lanes)
            weights = [spread(weight_rows[k : k + 1, here]) for k in range(taps)]
            for start in range(0, cap, piece):
                base = (j * cap + start).astype(f32)
                near = [spread(slot_rows[k : k + 1, here] - base) for k in range(taps)]
                for g in range(0, min(piece, cap), tile):
                    step_ids = ids + jnp.asarray(g, bf16)
                    total = None
                    for k in range(taps):
                        part = jnp.where(step_ids == near[k], weights[k], zero)
                        total = part if total is None else total + part
                    mix[j, start + g : start + g + tile, here] = total

    @pl.loop(0, EARLY)
    def _(j):
        mix_block(j)

    def picked(dest):
        asked = jnp.concatenate(
            [reqs[dest, part : part + 1, :] for part in range(parts)], axis=1
        ).astype(f32)
        ids = ladder(cap)
        rows = []
        for start in range(0, cells, piece):
            near = spread(asked - float(start))
            for g in range(0, piece, tile):
                rows.append(jnp.where(ids + jnp.asarray(g, bf16) == near, one, zero))
        hot = jnp.concatenate(rows, axis=0)
        return jnp.dot(src_t[...], hot, preferred_element_type=f32).astype(bf16)

    def post(step, sender, b):
        part = slice(b * FIELDS, (b + 1) * FIELDS)
        return pltpu.make_async_remote_copy(
            src_ref=outbox.at[step, part],
            dst_ref=inbox.at[sender, part],
            send_sem=box_send.at[b, step],
            recv_sem=box_recv.at[b, sender],
            device_id=(row, partner(step, 1)),
            device_id_type=MESH,
        )

    @pl.loop(1, n)
    def _(i):
        step = n - i
        dest = partner(step, 1)
        ask(step, dest).wait_recv()
        outbox[step] = picked(dest)
        post(step, me, 0).start()

    @pl.loop(1, n)
    def _(i):
        post(n - i, me, 1).start()

    inbox[me] = picked(me)

    @pl.loop(EARLY, n)
    def _(j):
        mix_block(j)

    def gather(b):
        part = slice(b * FIELDS, (b + 1) * FIELDS)
        post(1, partner(1, -1), b).wait_recv()
        total = jnp.dot(inbox[me, part], mix[me], preferred_element_type=f32)
        beside = partner(1, -1)
        acc[...] = total + jnp.dot(inbox[beside, part], mix[beside], preferred_element_type=f32)

        @pl.loop(1, n // 2)
        def _(i):
            senders = []
            for step in (n - 2 * i + 1, n - 2 * i):
                sender = partner(step, -1)
                post(step, sender, b).wait_recv()
                senders.append(sender)
            left, right = [
                jnp.dot(inbox[sender, part], mix[sender], preferred_element_type=f32)
                for sender in senders
            ]
            acc[...] += left + right

        turned = jnp.concatenate([acc[:, : spots // 2], acc[:, spots // 2 :]], axis=0).T.astype(bf16)
        for xb in range(blocks):
            pad[b, xb + 1, edge : edge + inner] = turned[xb * inner : (xb + 1) * inner]

        @pl.when(jnp.logical_not(has_up))
        def _():
            pad[b, :, :edge] = jnp.zeros((blocks + 2, edge, CH), bf16)

        @pl.when(jnp.logical_not(has_down))
        def _():
            pad[b, :, edge + inner :] = jnp.zeros((blocks + 2, edge, CH), bf16)

    mid = slice(edge, edge + inner)
    first, last = slice(edge, 2 * edge), slice(inner, inner + edge)
    low, high = slice(0, edge), slice(edge + inner, 2 * edge + inner)
    every = slice(1, blocks + 1)
    left, right = slice(1, 2), slice(blocks, blocks + 1)
    before, after = slice(0, 1), slice(blocks + 1, blocks + 2)
    moves = [
        (0, 1, (right, mid), (before, mid)),
        (0, -1, (left, mid), (after, mid)),
        (1, 0, (every, last), (every, low)),
        (1, 1, (right, last), (before, low)),
        (1, -1, (left, last), (after, low)),
        (-1, 0, (every, first), (every, high)),
        (-1, 1, (right, first), (before, high)),
        (-1, -1, (left, first), (after, high)),
    ]

    def shift(i, b):
        dr, dc, src, dst = moves[i]
        return pltpu.make_async_remote_copy(
            src_ref=pad.at[b, src[0], src[1]],
            dst_ref=pad.at[b, dst[0], dst[1]],
            send_sem=halo_send.at[b, i],
            recv_sem=halo_recv.at[b, i],
            device_id=(row + dr, lax.rem(me + dc + n, n)),
            device_id_type=MESH,
        )

    def halo_start(b):
        @pl.when(has_down)
        def _():
            for i in (2, 3, 4):
                shift(i, b).start()

        @pl.when(has_up)
        def _():
            for i in (5, 6, 7):
                shift(i, b).start()

        for i in (0, 1):
            shift(i, b).start()

    def halo_here(b):
        for i in (0, 1):
            shift(i, b).wait_recv()

        @pl.when(has_up)
        def _():
            for i in (2, 3, 4):
                shift(i, b).wait_recv()

        @pl.when(has_down)
        def _():
            for i in (5, 6, 7):
                shift(i, b).wait_recv()

    def sent():
        @pl.loop(1, n)
        def _(step):
            ask(step, me).wait_send()
            for b in range(2):
                post(step, me, b).wait_send()

        for b in range(2):
            for i in (0, 1):
                shift(i, b).wait_send()

        @pl.when(has_down)
        def _():
            for b in range(2):
                for i in (2, 3, 4):
                    shift(i, b).wait_send()

        @pl.when(has_up)
        def _():
            for b in range(2):
                for i in (5, 6, 7):
                    shift(i, b).wait_send()

    gather(0)
    halo_start(0)
    weights_ready()
    gather(1)
    halo_start(1)
    return halo_here, sent


def forward(source, wanted, stencil, weight, weights, tile_rows, tile_cols):
    n, cap = wanted.shape
    cells, columns = source.shape
    spots = tile_rows * tile_cols
    blocks = tile_cols // HALO
    rows = tile_rows + 2 * HALO
    taps = stencil.shape[0] // tile_rows
    dma = pltpu.SemaphoreType.DMA
    return pl.pallas_call(
        functools.partial(whole_kernel, tile_rows, tile_cols),
        out_shape=[
            pltpu.VMEM(shape, bf16)
            for shape in ((tile_rows + 2, tile_cols, 4 * CH), (12 * CH, 2 * CH), (2 * CH, 2 * CH))
        ],
        in_specs=[pl.BlockSpec(memory_space=pltpu.HBM)] * 11,
        out_specs=[pl.BlockSpec(memory_space=pltpu.VMEM)] * 3,
        scratch_shapes=[pltpu.VMEM(w.shape, bf16) for w in weights]
        + [dma((7,))]
        + weight_scratch()
        + [
            pltpu.VMEM((2, blocks + 2, rows * HALO // 2, columns), bf16),
            pltpu.VMEM(source.shape, bf16),
            pltpu.VMEM(wanted.shape, jnp.int32),
            pltpu.VMEM(stencil.shape, jnp.int32),
            pltpu.VMEM(weight.shape, f32),
            dma((4,)),
            pltpu.VMEM((n, cap // CH, CH), jnp.int32),
            pltpu.VMEM((n, cap // CH, CH), jnp.int32),
            pltpu.VMEM((columns, cells), bf16),
            pltpu.VMEM((n, cap, spots), bf16),
            pltpu.VMEM((n, columns, cap), bf16),
            pltpu.VMEM((n, columns, cap), bf16),
            pltpu.VMEM((FIELDS, spots), f32),
            pltpu.VMEM((taps, spots), f32),
            pltpu.VMEM((taps, spots), f32),
            dma((n,)), dma((n,)), dma((2, n)), dma((2, n)), dma((2, 8)), dma((2, 8)),
        ]
        + unet_scratch(tile_rows, tile_cols),
        compiler_params=pltpu.CompilerParams(
            collective_id=0, has_side_effects=True, vmem_limit_bytes=40 * 1024 * 1024
        ),
        cost_estimate=pl.CostEstimate(
            flops=10**9, bytes_accessed=2 * 10**6, transcendentals=0
        ),
    )(*[pltpu.with_memory_space_constraint(a, pltpu.HBM) for a in (source, wanted, stencil, weight, *weights)])


def body(source_tiles, requests, stencil, regrid_weight, *weights):
    tile_rows, tile_cols, taps = stencil.shape
    cells, columns = source_tiles.shape[2:]
    done = forward(
        source_tiles.reshape(cells, columns),
        requests.reshape(requests.shape[2:]),
        stencil.transpose(0, 2, 1).reshape(tile_rows * taps, tile_cols),
        regrid_weight.transpose(0, 2, 1).reshape(tile_rows * taps, tile_cols),
        (*weights[:-1], weights[-1].T),
        tile_rows,
        tile_cols,
    )
    return tail(*done).reshape(tile_rows, tile_cols, 2, FIELDS)


def solution(mesh):
    placed = (P("row", "col", None, None),) * 2 + (P("row", "col", None),) * 2 + (P(),) * 7
    return jax.shard_map(
        body, mesh=mesh, in_specs=placed, out_specs=P("row", "col", None, None), check_vma=False
    )
```

```python
import functools

import jax
import jax.numpy as jnp
from jax import lax
from jax.experimental import pallas as pl
from jax.experimental.pallas import tpu as pltpu
from jax.sharding import PartitionSpec as P

FIELDS = 64
CH = 128
HALO = 8
f32, bf16 = jnp.float32, jnp.bfloat16
MESH = pl.DeviceIdType.MESH


def silu(a):
    return a + a * jnp.tanh(a)


def halved(w):
    return (w.astype(f32) * 0.5).astype(bf16)


def pair_weight(out, base, w, dy):
    zero = jnp.zeros((CH, CH), bf16)
    left, middle, right = [halved(w[dy, dx]) for dx in range(3)]
    rows = [(middle, left), (right, middle), (left, zero), (zero, right)]
    for i, (even, odd) in enumerate(rows):
        place = slice(base + i * CH, base + (i + 1) * CH)
        out[place, :CH] = even
        out[place, CH:] = odd


def prepare(w_in, w_enc, w_m1, w_m2, w_d1, w_d2, w_out, c_in, c_enc, c_m1, c_m2, c_d1, c_d2, c_out):
    quad = 4 * FIELDS
    none = jnp.zeros((FIELDS, CH), bf16)
    for dy in range(3):
        for j in range(4):
            place = slice(dy * quad + j * FIELDS, dy * quad + (j + 1) * FIELDS)
            c_in[place, :CH] = halved(w_in[dy, j]) if j < 3 else none
            c_in[place, CH:] = halved(w_in[dy, j - 1]) if j > 0 else none
        base = dy * 4 * CH
        pair_weight(c_enc, base, w_enc, dy)
        pair_weight(c_m1, base, w_m1, dy)
        pair_weight(c_m2, base, w_m2, dy)
        pair_weight(c_d2, base, w_d2, dy)
        for par in range(2):
            pair_weight(c_d1.at[par], base, w_d1.at[:, :, CH:], dy)
    zero = jnp.zeros((CH, CH), bf16)
    for par in range(2):
        groups = ((0, 1), (2,)) if par == 0 else ((0,), (1, 2))
        for g, dys in enumerate(groups):
            taps = [0.5 * sum(w_d1[dy, dx, :CH].astype(f32) for dy in dys) for dx in range(3)]
            base = 12 * CH + g * 3 * CH
            rows = [
                (taps[0].astype(bf16), zero),
                ((taps[1] + taps[2]).astype(bf16), (taps[0] + taps[1]).astype(bf16)),
                (zero, taps[2].astype(bf16)),
            ]
            for i, (even, odd) in enumerate(rows):
                place = slice(base + i * CH, base + (i + 1) * CH)
                c_d1[par, place, :CH] = even
                c_d1[par, place, CH:] = odd
    last = w_out[...].astype(f32).T.astype(bf16)
    pad = jnp.zeros((CH, CH - FIELDS), bf16)
    full = jnp.concatenate([last.astype(f32), pad.astype(f32)], axis=1).astype(bf16)
    c_out[:CH, :CH] = full
    c_out[CH:, CH:] = full
    c_out[:CH, CH:] = zero
    c_out[CH:, :CH] = zero


def split(total, parts):
    size = -(-total // (2 * parts)) * 2
    return [(at, min(size, total - at)) for at in range(0, total, size)]


FIRST_CHUNKS, SKIP_CHUNKS = 2, 2


def pairs_of(tile_cols):
    return tile_cols // 2 + HALO


def unet_body(tile_rows, tile_cols, at_top, at_bottom, halo_here, pad, weights, dec, quad, first, skip, tmp, pooled, middle, up, part):
    c_in, c_enc, c_m1, c_m2, c_d1 = weights
    rows = tile_rows + 2 * HALO
    pairs = pairs_of(tile_cols)
    line = 2 * pairs
    half = line // 2
    h_first, h_skip = tile_rows + 14, tile_rows + 12
    h_pool = h_skip // 2
    h_mid, h_coarse = h_pool - 2, h_pool - 4
    h_dec = (tile_rows + 2) // 2
    own = tile_cols // 2
    top_scale = jnp.where(at_top, 0.0, 1.0).astype(f32)
    bottom_scale = jnp.where(at_bottom, 0.0, 1.0).astype(f32)
    low = lax.broadcasted_iota(jnp.int32, (1, CH), 1) < FIELDS
    upper = lax.broadcasted_iota(jnp.int32, (1, 8, 1), 1) < 4
    groups = pairs // 8

    def rolled(value, by):
        return pltpu.roll(value, by % value.shape[0], 0)

    def line_up(b):
        parts = []
        for g in range(groups):
            x, y = [
                pad[b, 2 * g + i].astype(f32).reshape(rows // 2, 8, CH) for i in range(2)
            ]
            turned_x, turned_y = pltpu.roll(x, 4, 1), pltpu.roll(y, 4, 1)
            both = jnp.stack(
                [jnp.where(upper, x, turned_y), jnp.where(upper, turned_x, y)], axis=1
            )
            parts.append(both.reshape(rows, 8, CH))
        value = jnp.concatenate(parts, axis=1).reshape(rows * pairs, CH)
        value = pltpu.roll(value, FIELDS, 1)
        value = jnp.concatenate(
            [
                jnp.where(low, rolled(value, 1), value),
                jnp.where(low, value, rolled(value, -1)),
            ],
            axis=1,
        )
        keep(quad, b, 0, value)

    def keep(ref, b, at, value):
        place = slice(at * pairs, at * pairs + value.shape[0])
        ref[b, 0, place] = value.astype(bf16)
        if at == 0:
            ref[b, 1, : value.shape[0] - pairs] = value[pairs:].astype(bf16)
        else:
            ref[b, 1, place.start - pairs : place.stop - pairs] = value.astype(bf16)

    def three(ref, b, at, count):
        start, size = at * pairs, count * pairs
        return [
            ref[b, 0, start : start + size],
            ref[b, 1, start : start + size],
            ref[b, 0, start + 2 * pairs : start + 2 * pairs + size],
        ]

    def inside(value, at, count, depth, total, width):
        above = max(0, min(depth, at + count) - at) * width
        below = max(0, at + count - max(at, total - depth)) * width
        parts = [value[:above] * top_scale] if above else []
        parts.append(value[above : value.shape[0] - below])
        if below:
            parts.append(value[value.shape[0] - below :] * bottom_scale)
        return jnp.concatenate(parts, axis=0)

    def dot(windows, weight):
        return silu(
            jnp.dot(jnp.concatenate(windows, axis=1), weight, preferred_element_type=f32)
        )

    def sides(value):
        return jnp.concatenate([rolled(value[:, CH:], 1), rolled(value[:, :CH], -1)], axis=1)

    def window(ref, start, count, width, dy):
        return ref[pl.ds(pl.multiple_of((start + dy) * width, 8), count * width), :]

    def encode(b):
        line_up(b)
        for at, count in split(h_first, FIRST_CHUNKS):
            v = dot(three(quad, b, at, count), c_in[...])
            v = inside(v, at, count, 7, h_first, pairs)
            keep(first, b, at, jnp.concatenate([v, sides(v)], axis=1))
        for at, count in split(h_skip, SKIP_CHUNKS):
            v = dot(three(first, b, at, count), c_enc[...])
            v = inside(v, at, count, 6, h_skip, pairs)
            half_rows = count // 2
            both = jnp.concatenate([v, sides(v)], axis=1).reshape(half_rows, 2, pairs, 4 * CH)
            for par in range(2):
                piece = both[:, par].reshape(half_rows * pairs, 4 * CH)
                place = at // 2 * pairs
                skip[b, 0, par, place : place + half_rows * pairs] = piece.astype(bf16)
                if at == 0:
                    piece = piece[pairs:]
                else:
                    place -= pairs
                skip[b, 1, par, place : place + piece.shape[0]] = piece.astype(bf16)
            v = v.reshape(half_rows, 2 * pairs, 2 * CH)
            v = v[:, :pairs] + v[:, pairs:]
            v = (v[:, :, :CH] + v[:, :, CH:]) * 0.25
            for t in range(half_rows):
                place = (at // 2 + t) * line + b * pairs
                tmp[place : place + pairs, :] = v[t]
        for par in range(2):
            size = h_dec * pairs
            windows = [
                skip[b, d // 2, d % 2, 2 * pairs : 2 * pairs + size] for d in range(par, par + 3)
            ]
            part[b, par] = jnp.dot(
                jnp.concatenate(windows, axis=1), c_d1[par, : 12 * CH], preferred_element_type=f32
            )

    for b in range(2):
        halo_here(b)
        encode(b)

    size = h_pool * half
    v = jnp.concatenate([tmp[pl.ds(0, size, stride=2), :], tmp[pl.ds(1, size, stride=2), :]], axis=1)
    pooled[...] = jnp.concatenate([v, sides(v)], axis=1)

    v = dot([window(pooled, 0, h_mid, half, dy).astype(bf16) for dy in range(3)], c_m1[...])
    v = inside(v, 0, h_mid, 2, h_mid, half)
    middle[...] = jnp.concatenate([v, sides(v)], axis=1)

    v = dot([window(middle, 0, h_coarse, half, dy).astype(bf16) for dy in range(3)], c_m2[...])
    size = h_coarse * half
    tmp[pl.ds(0, size, stride=2), :] = v[:, :CH]
    tmp[pl.ds(1, size, stride=2), :] = v[:, CH:]
    v = inside(tmp[: 2 * size, :], 0, h_coarse, 1, h_coarse, line)
    v = jnp.concatenate([rolled(v, 1), v, rolled(v, -1)], axis=1).reshape(h_coarse, line, 3 * CH)
    for b in range(2):
        piece = v[:, b * pairs : (b + 1) * pairs].reshape(h_coarse * pairs, 3 * CH)
        up[b] = jnp.concatenate([piece[:-pairs], piece[pairs:]], axis=1).astype(bf16)

    def compact(value):
        value = value.reshape(h_dec, groups, 8, value.shape[1])
        turned = [pltpu.roll(value[:, g], 4, 1) for g in range(groups)]
        parts = [jnp.where(upper, turned[g], turned[g + 1]) for g in range(groups - 1)]
        return jnp.concatenate(parts, axis=1)

    for b in range(2):
        for par in range(2):
            v = part[b, par] + jnp.dot(up[b], c_d1[par, 12 * CH :], preferred_element_type=f32)
            v = silu(v)
            if par == 0:
                v = jnp.concatenate([v[:pairs] * top_scale, v[pairs:]], axis=0)
            else:
                v = jnp.concatenate([v[:-pairs], v[-pairs:] * bottom_scale], axis=0)
            both = jnp.concatenate([compact(v), compact(sides(v))], axis=2).astype(bf16)
            for i in range(h_dec):
                dec[2 * i + par, b * own : (b + 1) * own] = both[i]


def tail_body(tile_rows, own, dec, c_d2, c_out, last, put):
    n = tile_rows // TAIL_CHUNKS
    for i in range(TAIL_CHUNKS):
        windows = [
            dec[i * n + dy : (i + 1) * n + dy].reshape(n * 2 * own, 4 * CH) for dy in range(3)
        ]
        v = silu(
            jnp.dot(jnp.concatenate(windows, axis=1), c_d2[...], preferred_element_type=f32)
        )
        z = jnp.dot(v.astype(bf16), c_out[...], preferred_element_type=f32)
        z = z.reshape(n, 2 * own, 2 * CH)
        for px in range(2):
            for b in range(2):
                piece = z[:, b * own : (b + 1) * own, px * CH : (px + 1) * CH]
                last[pl.ds(i * n * own * 4 + 2 * px + b, n * own, stride=4), :] = piece.reshape(n * own, CH)
        put(i * n * own * 4, n * own * 4)


TAIL_CHUNKS = 1


def unet_scratch(tile_rows, tile_cols):
    line = 2 * pairs_of(tile_cols)
    half = line // 2
    h_pool = (tile_rows + 12) // 2
    return [
        pltpu.VMEM((2, 2, (tile_rows + 2 * HALO) * half, 2 * CH), bf16),
        pltpu.VMEM((2, 2, (tile_rows + 14) * half, 4 * CH), bf16),
        pltpu.VMEM((2, 2, 2, h_pool * half, 4 * CH), bf16),
        pltpu.VMEM((h_pool * line, CH), f32),
        pltpu.VMEM((h_pool * half, 4 * CH), f32),
        pltpu.VMEM(((h_pool - 2) * half, 4 * CH), f32),
        pltpu.VMEM((2, (h_pool - 5) * half, 6 * CH), bf16),
        pltpu.VMEM((2, 2, (h_pool - 5) * half, 2 * CH), f32),
    ]


def weight_scratch():
    square = pltpu.VMEM((12 * CH, 2 * CH), bf16)
    return [
        pltpu.VMEM((12 * FIELDS, 2 * CH), bf16), square, square, square,
        pltpu.VMEM((2, 18 * CH, 2 * CH), bf16),
    ]


def whole_kernel(tile_rows, tile_cols, *refs):
    ins, w_hbm, out_ref, scratch = refs[:4], refs[4:11], refs[11], refs[12:]
    w_vmem, w_sem, mats = scratch[:7], scratch[7], scratch[8:13]
    pad, own, unet_refs = scratch[13], scratch[14:34], scratch[34:-4]
    dec, c_d2, c_out, last = scratch[-4:]

    def weights_start():
        for i in range(7):
            pltpu.make_async_copy(w_hbm[i], w_vmem[i], w_sem.at[i]).start()

    def weights_ready():
        for i in range(7):
            pltpu.make_async_copy(w_hbm[i], w_vmem[i], w_sem.at[i]).wait()
        prepare(*w_vmem, *mats, c_d2, c_out)

    halo_here, sent = regrid_body(
        tile_rows, tile_cols, weights_start, weights_ready, *ins, pad, *own
    )
    row = lax.axis_index("row")
    unet_body(
        tile_rows, tile_cols, row == 0, row == lax.axis_size("row") - 1,
        halo_here, pad, mats, dec, *unet_refs,
    )

    def put(start, count):
        place = slice(start, start + count)
        out_ref[place, :] = last[place, :FIELDS].astype(bf16)

    tail_body(tile_rows, tile_cols // 2, dec, c_d2, c_out, last, put)
    sent()


def write_kernel(value, out_ref, sem):
    copy = pltpu.make_async_copy(value, out_ref, sem)
    copy.start()
    copy.wait()


def write(value):
    return pl.pallas_call(
        write_kernel,
        out_shape=jax.ShapeDtypeStruct(value.shape, bf16),
        in_specs=[pl.BlockSpec(memory_space=pltpu.VMEM)],
        out_specs=pl.BlockSpec(memory_space=pltpu.HBM),
        scratch_shapes=[pltpu.SemaphoreType.DMA],
    )(pltpu.with_memory_space_constraint(value, pltpu.VMEM))


EARLY = 0


def regrid_body(
    tile_rows, tile_cols, weights_start, weights_ready, src_in, req_in, sten_in, wgt_in, pad,
    src_ref, req_ref, sten_ref, wgt_ref, load, asks, reqs, src_t, mix, outbox, inbox, acc, slot_rows, weight_rows,
    req_send, req_recv, box_send, box_recv, halo_send, halo_recv,
):
    row, me = lax.axis_index("row"), lax.axis_index("col")
    n_row, n = lax.axis_size("row"), lax.axis_size("col")
    cap = req_ref.shape[1]
    cells = src_ref.shape[0]
    spots = tile_rows * tile_cols
    has_up, has_down = row > 0, row < n_row - 1
    wide = HALO // 2
    blocks = tile_cols // HALO
    edge = HALO * wide
    inner = tile_rows * wide

    loads = [
        pltpu.make_async_copy(outer, held, load.at[i])
        for i, (outer, held) in enumerate(
            [(req_in, req_ref), (src_in, src_ref), (sten_in, sten_ref), (wgt_in, wgt_ref)]
        )
    ]
    for copy in loads:
        copy.start()

    barrier = pltpu.get_barrier_semaphore()

    def greet(r, c):
        pl.semaphore_signal(
            barrier, inc=1, device_id=(r, lax.rem(c + n, n)), device_id_type=MESH
        )

    @pl.loop(1, n)
    def _(step):
        greet(row, me + step)

    @pl.when(has_up)
    def _():
        for d in (-1, 0, 1):
            greet(row - 1, me + d)

    @pl.when(has_down)
    def _():
        for d in (-1, 0, 1):
            greet(row + 1, me + d)

    weights_start()
    loads[0].wait()
    parts = cap // CH
    for j in range(n):
        for part in range(parts):
            asks[j, part : part + 1, :] = req_ref[j : j + 1, part * CH : (part + 1) * CH]

    rows_beside = jnp.minimum(row, 1) + jnp.minimum(n_row - 1 - row, 1)
    pl.semaphore_wait(barrier, n - 1 + 3 * rows_beside)

    def partner(step, sign):
        chip = lax.rem(me // 2 + sign * (step // 2) + n, n // 2)
        return chip * 2 + lax.rem(me + step, 2)

    def ask(step, sender):
        dest = partner(step, 1)
        return pltpu.make_async_remote_copy(
            src_ref=asks.at[dest],
            dst_ref=reqs.at[sender],
            send_sem=req_send.at[step],
            recv_sem=req_recv.at[sender],
            device_id=(row, dest),
            device_id_type=MESH,
        )

    @pl.loop(1, n)
    def _(i):
        ask(n - i, me).start()

    reqs[me] = asks[me]
    loads[1].wait()
    src_t[...] = src_ref[...].astype(f32).T.astype(bf16)

    loads[2].wait()
    loads[3].wait()
    taps = sten_ref.shape[0] // tile_rows
    lane = lax.broadcasted_iota(jnp.int32, (tile_cols, spots), 1)
    cell = lax.broadcasted_iota(jnp.int32, (tile_cols, spots), 0)
    column = lane // (spots // 2) + lane % wide * 2 + lane // inner % blocks * HALO
    turn = jnp.where(cell == column, 1.0, 0.0).astype(bf16)
    held = tile_rows * taps
    mine = lax.broadcasted_iota(jnp.int32, (held, spots), 0) // taps == (
        lax.broadcasted_iota(jnp.int32, (held, spots), 1) // wide % tile_rows
    )

    def in_order(values):
        spread = jnp.dot(values.astype(bf16), turn, preferred_element_type=f32)
        spread = jnp.where(mine, spread, 0.0).reshape(held // 8, 8, spots)
        total = jnp.sum(spread, axis=0)
        return total[:taps] + total[taps:]

    slots = sten_ref[...]
    slot_rows[...] = in_order((slots // 256).astype(f32)) * 256.0 + in_order((slots % 256).astype(f32))
    weight_rows[...] = in_order(wgt_ref[...])
    tile, piece = 16, 256

    def ladder(width):
        return lax.broadcasted_iota(jnp.int32, (tile, width), 0).astype(f32).astype(bf16)

    def spread(values):
        return jnp.broadcast_to(values, (tile, values.shape[1])).astype(bf16)

    lanes = min(512, spots)
    zero, one = jnp.zeros((), bf16), jnp.ones((), bf16)

    def mix_block(j):
        for left_lane in range(0, spots, lanes):
            here = slice(left_lane, left_lane + lanes)
            ids = ladder(lanes)
            weights = [spread(weight_rows[k : k + 1, here]) for k in range(taps)]
            for start in range(0, cap, piece):
                base = (j * cap + start).astype(f32)
                near = [spread(slot_rows[k : k + 1, here] - base) for k in range(taps)]
                for g in range(0, min(piece, cap), tile):
                    step_ids = ids + jnp.asarray(g, bf16)
                    total = None
                    for k in range(taps):
                        part = jnp.where(step_ids == near[k], weights[k], zero)
                        total = part if total is None else total + part
                    mix[j, start + g : start + g + tile, here] = total

    @pl.loop(0, EARLY)
    def _(j):
        mix_block(j)

    def picked(dest):
        asked = jnp.concatenate(
            [reqs[dest, part : part + 1, :] for part in range(parts)], axis=1
        ).astype(f32)
        ids = ladder(cap)
        rows = []
        for start in range(0, cells, piece):
            near = spread(asked - float(start))
            for g in range(0, piece, tile):
                rows.append(jnp.where(ids + jnp.asarray(g, bf16) == near, one, zero))
        hot = jnp.concatenate(rows, axis=0)
        return jnp.dot(src_t[...], hot, preferred_element_type=f32).astype(bf16)

    def post(step, sender, b):
        part = slice(b * FIELDS, (b + 1) * FIELDS)
        return pltpu.make_async_remote_copy(
            src_ref=outbox.at[step, part],
            dst_ref=inbox.at[sender, part],
            send_sem=box_send.at[b, step],
            recv_sem=box_recv.at[b, sender],
            device_id=(row, partner(step, 1)),
            device_id_type=MESH,
        )

    @pl.loop(1, n)
    def _(i):
        step = n - i
        dest = partner(step, 1)
        ask(step, dest).wait_recv()
        outbox[step] = picked(dest)
        post(step, me, 0).start()

    @pl.loop(1, n)
    def _(i):
        post(n - i, me, 1).start()

    inbox[me] = picked(me)

    @pl.loop(EARLY, n)
    def _(j):
        mix_block(j)

    def gather(b):
        part = slice(b * FIELDS, (b + 1) * FIELDS)
        post(1, partner(1, -1), b).wait_recv()
        total = jnp.dot(inbox[me, part], mix[me], preferred_element_type=f32)
        beside = partner(1, -1)
        acc[...] = total + jnp.dot(inbox[beside, part], mix[beside], preferred_element_type=f32)

        @pl.loop(1, n // 2)
        def _(i):
            senders = []
            for step in (n - 2 * i + 1, n - 2 * i):
                sender = partner(step, -1)
                post(step, sender, b).wait_recv()
                senders.append(sender)
            left, right = [
                jnp.dot(inbox[sender, part], mix[sender], preferred_element_type=f32)
                for sender in senders
            ]
            acc[...] += left + right

        turned = jnp.concatenate([acc[:, : spots // 2], acc[:, spots // 2 :]], axis=0).T.astype(bf16)
        for xb in range(blocks):
            pad[b, xb + 1, edge : edge + inner] = turned[xb * inner : (xb + 1) * inner]

        @pl.when(jnp.logical_not(has_up))
        def _():
            pad[b, :, :edge] = jnp.zeros((blocks + 2, edge, CH), bf16)

        @pl.when(jnp.logical_not(has_down))
        def _():
            pad[b, :, edge + inner :] = jnp.zeros((blocks + 2, edge, CH), bf16)

    mid = slice(edge, edge + inner)
    first, last = slice(edge, 2 * edge), slice(inner, inner + edge)
    low, high = slice(0, edge), slice(edge + inner, 2 * edge + inner)
    every = slice(1, blocks + 1)
    left, right = slice(1, 2), slice(blocks, blocks + 1)
    before, after = slice(0, 1), slice(blocks + 1, blocks + 2)
    moves = [
        (0, 1, (right, mid), (before, mid)),
        (0, -1, (left, mid), (after, mid)),
        (1, 0, (every, last), (every, low)),
        (1, 1, (right, last), (before, low)),
        (1, -1, (left, last), (after, low)),
        (-1, 0, (every, first), (every, high)),
        (-1, 1, (right, first), (before, high)),
        (-1, -1, (left, first), (after, high)),
    ]

    def shift(i, b):
        dr, dc, src, dst = moves[i]
        return pltpu.make_async_remote_copy(
            src_ref=pad.at[b, src[0], src[1]],
            dst_ref=pad.at[b, dst[0], dst[1]],
            send_sem=halo_send.at[b, i],
            recv_sem=halo_recv.at[b, i],
            device_id=(row + dr, lax.rem(me + dc + n, n)),
            device_id_type=MESH,
        )

    def halo_start(b):
        @pl.when(has_down)
        def _():
            for i in (2, 3, 4):
                shift(i, b).start()

        @pl.when(has_up)
        def _():
            for i in (5, 6, 7):
                shift(i, b).start()

        for i in (0, 1):
            shift(i, b).start()

    def halo_here(b):
        for i in (0, 1):
            shift(i, b).wait_recv()

        @pl.when(has_up)
        def _():
            for i in (2, 3, 4):
                shift(i, b).wait_recv()

        @pl.when(has_down)
        def _():
            for i in (5, 6, 7):
                shift(i, b).wait_recv()

    def sent():
        @pl.loop(1, n)
        def _(step):
            ask(step, me).wait_send()
            for b in range(2):
                post(step, me, b).wait_send()

        for b in range(2):
            for i in (0, 1):
                shift(i, b).wait_send()

        @pl.when(has_down)
        def _():
            for b in range(2):
                for i in (2, 3, 4):
                    shift(i, b).wait_send()

        @pl.when(has_up)
        def _():
            for b in range(2):
                for i in (5, 6, 7):
                    shift(i, b).wait_send()

    gather(0)
    halo_start(0)
    weights_ready()
    gather(1)
    halo_start(1)
    return halo_here, sent


def forward(source, wanted, stencil, weight, weights, tile_rows, tile_cols):
    n, cap = wanted.shape
    cells, columns = source.shape
    spots = tile_rows * tile_cols
    blocks = tile_cols // HALO
    rows = tile_rows + 2 * HALO
    taps = stencil.shape[0] // tile_rows
    dma = pltpu.SemaphoreType.DMA
    return pl.pallas_call(
        functools.partial(whole_kernel, tile_rows, tile_cols),
        out_shape=pltpu.VMEM((2 * spots, FIELDS), bf16),
        in_specs=[pl.BlockSpec(memory_space=pltpu.HBM)] * 11,
        out_specs=pl.BlockSpec(memory_space=pltpu.VMEM),
        scratch_shapes=[pltpu.VMEM(w.shape, bf16) for w in weights]
        + [dma((7,))]
        + weight_scratch()
        + [
            pltpu.VMEM((2, blocks + 2, rows * HALO // 2, columns), bf16),
            pltpu.VMEM(source.shape, bf16),
            pltpu.VMEM(wanted.shape, jnp.int32),
            pltpu.VMEM(stencil.shape, jnp.int32),
            pltpu.VMEM(weight.shape, f32),
            dma((4,)),
            pltpu.VMEM((n, cap // CH, CH), jnp.int32),
            pltpu.VMEM((n, cap // CH, CH), jnp.int32),
            pltpu.VMEM((columns, cells), bf16),
            pltpu.VMEM((n, cap, spots), bf16),
            pltpu.VMEM((n, columns, cap), bf16),
            pltpu.VMEM((n, columns, cap), bf16),
            pltpu.VMEM((FIELDS, spots), f32),
            pltpu.VMEM((taps, spots), f32),
            pltpu.VMEM((taps, spots), f32),
            dma((n,)), dma((n,)), dma((2, n)), dma((2, n)), dma((2, 8)), dma((2, 8)),
        ]
        + unet_scratch(tile_rows, tile_cols)
        + [
            pltpu.VMEM((tile_rows + 2, tile_cols, 4 * CH), bf16),
            pltpu.VMEM((12 * CH, 2 * CH), bf16),
            pltpu.VMEM((2 * CH, 2 * CH), bf16),
            pltpu.VMEM((2 * spots, CH), f32),
        ],
        compiler_params=pltpu.CompilerParams(
            collective_id=0, has_side_effects=True, vmem_limit_bytes=40 * 1024 * 1024
        ),
        cost_estimate=pl.CostEstimate(
            flops=10**9, bytes_accessed=2 * 10**6, transcendentals=0
        ),
    )(*[pltpu.with_memory_space_constraint(a, pltpu.HBM) for a in (source, wanted, stencil, weight, *weights)])


def body(source_tiles, requests, stencil, regrid_weight, *weights):
    tile_rows, tile_cols, taps = stencil.shape
    cells, columns = source_tiles.shape[2:]
    done = forward(
        source_tiles.reshape(cells, columns),
        requests.reshape(requests.shape[2:]),
        stencil.transpose(0, 2, 1).reshape(tile_rows * taps, tile_cols),
        regrid_weight.transpose(0, 2, 1).reshape(tile_rows * taps, tile_cols),
        (*weights[:-1], weights[-1].T),
        tile_rows,
        tile_cols,
    )
    return write(done).reshape(tile_rows, tile_cols, 2, FIELDS)


def solution(mesh):
    placed = (P("row", "col", None, None),) * 2 + (P("row", "col", None),) * 2 + (P(),) * 7
    return jax.shard_map(
        body, mesh=mesh, in_specs=placed, out_specs=P("row", "col", None, None), check_vma=False
    )
```

```python
import functools

import jax
import jax.numpy as jnp
from jax import lax
from jax.experimental import pallas as pl
from jax.experimental.pallas import tpu as pltpu
from jax.sharding import PartitionSpec as P

FIELDS = 64
CH = 128
HALO = 8
f32, bf16 = jnp.float32, jnp.bfloat16
MESH = pl.DeviceIdType.MESH


def silu(a):
    return a + a * jnp.tanh(a)


def halved(w):
    return (w.astype(f32) * 0.5).astype(bf16)


def pair_weight(out, base, w, dy):
    zero = jnp.zeros((CH, CH), bf16)
    left, middle, right = [halved(w[dy, dx]) for dx in range(3)]
    rows = [(middle, left), (right, middle), (left, zero), (zero, right)]
    for i, (even, odd) in enumerate(rows):
        place = slice(base + i * CH, base + (i + 1) * CH)
        out[place, :CH] = even
        out[place, CH:] = odd


def prepare(w_in, w_enc, w_m1, w_m2, w_d1, w_d2, w_out, c_in, c_enc, c_m1, c_m2, c_d1, c_d2, c_out):
    quad = 4 * FIELDS
    none = jnp.zeros((FIELDS, CH), bf16)
    for dy in range(3):
        for j in range(4):
            place = slice(dy * quad + j * FIELDS, dy * quad + (j + 1) * FIELDS)
            c_in[place, :CH] = halved(w_in[dy, j]) if j < 3 else none
            c_in[place, CH:] = halved(w_in[dy, j - 1]) if j > 0 else none
        base = dy * 4 * CH
        pair_weight(c_enc, base, w_enc, dy)
        pair_weight(c_m1, base, w_m1, dy)
        pair_weight(c_m2, base, w_m2, dy)
        pair_weight(c_d2, base, w_d2, dy)
        for par in range(2):
            pair_weight(c_d1.at[par], base, w_d1.at[:, :, CH:], dy)
    zero = jnp.zeros((CH, CH), bf16)
    for par in range(2):
        groups = ((0, 1), (2,)) if par == 0 else ((0,), (1, 2))
        for g, dys in enumerate(groups):
            taps = [0.5 * sum(w_d1[dy, dx, :CH].astype(f32) for dy in dys) for dx in range(3)]
            base = 12 * CH + g * 3 * CH
            rows = [
                (taps[0].astype(bf16), zero),
                ((taps[1] + taps[2]).astype(bf16), (taps[0] + taps[1]).astype(bf16)),
                (zero, taps[2].astype(bf16)),
            ]
            for i, (even, odd) in enumerate(rows):
                place = slice(base + i * CH, base + (i + 1) * CH)
                c_d1[par, place, :CH] = even
                c_d1[par, place, CH:] = odd
    last = w_out[...].astype(f32).T.astype(bf16)
    pad = jnp.zeros((CH, CH - FIELDS), bf16)
    full = jnp.concatenate([last.astype(f32), pad.astype(f32)], axis=1).astype(bf16)
    c_out[:CH, :CH] = full
    c_out[CH:, CH:] = full
    c_out[:CH, CH:] = zero
    c_out[CH:, :CH] = zero


def split(total, parts):
    size = -(-total // (2 * parts)) * 2
    return [(at, min(size, total - at)) for at in range(0, total, size)]


FIRST_CHUNKS, SKIP_CHUNKS = 3, 2


def pairs_of(tile_cols):
    return tile_cols // 2 + HALO


def unet_body(tile_rows, tile_cols, at_top, at_bottom, halo_here, pad, weights, dec, quad, first, skip, tmp, pooled, middle, up, part):
    c_in, c_enc, c_m1, c_m2, c_d1 = weights
    rows = tile_rows + 2 * HALO
    pairs = pairs_of(tile_cols)
    line = 2 * pairs
    half = line // 2
    h_first, h_skip = tile_rows + 14, tile_rows + 12
    h_pool = h_skip // 2
    h_mid, h_coarse = h_pool - 2, h_pool - 4
    h_dec = (tile_rows + 2) // 2
    own = tile_cols // 2
    top_scale = jnp.where(at_top, 0.0, 1.0).astype(f32)
    bottom_scale = jnp.where(at_bottom, 0.0, 1.0).astype(f32)
    low = lax.broadcasted_iota(jnp.int32, (1, CH), 1) < FIELDS
    upper = lax.broadcasted_iota(jnp.int32, (1, 8, 1), 1) < 4
    groups = pairs // 8

    def rolled(value, by):
        return pltpu.roll(value, by % value.shape[0], 0)

    def line_up(b):
        parts = []
        for g in range(groups):
            x, y = [
                pad[b, 2 * g + i].astype(f32).reshape(rows // 2, 8, CH) for i in range(2)
            ]
            turned_x, turned_y = pltpu.roll(x, 4, 1), pltpu.roll(y, 4, 1)
            both = jnp.stack(
                [jnp.where(upper, x, turned_y), jnp.where(upper, turned_x, y)], axis=1
            )
            parts.append(both.reshape(rows, 8, CH))
        value = jnp.concatenate(parts, axis=1).reshape(rows * pairs, CH)
        value = pltpu.roll(value, FIELDS, 1)
        value = jnp.concatenate(
            [
                jnp.where(low, rolled(value, 1), value),
                jnp.where(low, value, rolled(value, -1)),
            ],
            axis=1,
        )
        keep(quad, b, 0, value)

    def keep(ref, b, at, value):
        place = slice(at * pairs, at * pairs + value.shape[0])
        ref[b, 0, place] = value.astype(bf16)
        if at == 0:
            ref[b, 1, : value.shape[0] - pairs] = value[pairs:].astype(bf16)
        else:
            ref[b, 1, place.start - pairs : place.stop - pairs] = value.astype(bf16)

    def three(ref, b, at, count):
        start, size = at * pairs, count * pairs
        return [
            ref[b, 0, start : start + size],
            ref[b, 1, start : start + size],
            ref[b, 0, start + 2 * pairs : start + 2 * pairs + size],
        ]

    def inside(value, at, count, depth, total, width):
        above = max(0, min(depth, at + count) - at) * width
        below = max(0, at + count - max(at, total - depth)) * width
        parts = [value[:above] * top_scale] if above else []
        parts.append(value[above : value.shape[0] - below])
        if below:
            parts.append(value[value.shape[0] - below :] * bottom_scale)
        return jnp.concatenate(parts, axis=0)

    def dot(windows, weight):
        return silu(
            jnp.dot(jnp.concatenate(windows, axis=1), weight, preferred_element_type=f32)
        )

    def sides(value):
        return jnp.concatenate([rolled(value[:, CH:], 1), rolled(value[:, :CH], -1)], axis=1)

    def window(ref, start, count, width, dy):
        return ref[pl.ds(pl.multiple_of((start + dy) * width, 8), count * width), :]

    def encode(b):
        line_up(b)
        for at, count in split(h_first, FIRST_CHUNKS):
            v = dot(three(quad, b, at, count), c_in[...])
            v = inside(v, at, count, 7, h_first, pairs)
            keep(first, b, at, jnp.concatenate([v, sides(v)], axis=1))
        for at, count in split(h_skip, SKIP_CHUNKS):
            v = dot(three(first, b, at, count), c_enc[...])
            v = inside(v, at, count, 6, h_skip, pairs)
            half_rows = count // 2
            both = jnp.concatenate([v, sides(v)], axis=1).reshape(half_rows, 2, pairs, 4 * CH)
            for par in range(2):
                piece = both[:, par].reshape(half_rows * pairs, 4 * CH)
                place = at // 2 * pairs
                skip[b, 0, par, place : place + half_rows * pairs] = piece.astype(bf16)
                if at == 0:
                    piece = piece[pairs:]
                else:
                    place -= pairs
                skip[b, 1, par, place : place + piece.shape[0]] = piece.astype(bf16)
            v = v.reshape(half_rows, 2 * pairs, 2 * CH)
            v = v[:, :pairs] + v[:, pairs:]
            v = (v[:, :, :CH] + v[:, :, CH:]) * 0.25
            for t in range(half_rows):
                place = (at // 2 + t) * line + b * pairs
                tmp[place : place + pairs, :] = v[t]
        for par in range(2):
            size = h_dec * pairs
            windows = [
                skip[b, d // 2, d % 2, 2 * pairs : 2 * pairs + size] for d in range(par, par + 3)
            ]
            part[b, par] = jnp.dot(
                jnp.concatenate(windows, axis=1), c_d1[par, : 12 * CH], preferred_element_type=f32
            )

    for b in range(2):
        halo_here(b)
        encode(b)

    size = h_pool * half
    v = jnp.concatenate([tmp[pl.ds(0, size, stride=2), :], tmp[pl.ds(1, size, stride=2), :]], axis=1)
    pooled[...] = jnp.concatenate([v, sides(v)], axis=1)

    v = dot([window(pooled, 0, h_mid, half, dy).astype(bf16) for dy in range(3)], c_m1[...])
    v = inside(v, 0, h_mid, 2, h_mid, half)
    middle[...] = jnp.concatenate([v, sides(v)], axis=1)

    v = dot([window(middle, 0, h_coarse, half, dy).astype(bf16) for dy in range(3)], c_m2[...])
    size = h_coarse * half
    tmp[pl.ds(0, size, stride=2), :] = v[:, :CH]
    tmp[pl.ds(1, size, stride=2), :] = v[:, CH:]
    v = inside(tmp[: 2 * size, :], 0, h_coarse, 1, h_coarse, line)
    v = jnp.concatenate([rolled(v, 1), v, rolled(v, -1)], axis=1).reshape(h_coarse, line, 3 * CH)
    for b in range(2):
        piece = v[:, b * pairs : (b + 1) * pairs].reshape(h_coarse * pairs, 3 * CH)
        up[b] = jnp.concatenate([piece[:-pairs], piece[pairs:]], axis=1).astype(bf16)

    def compact(value):
        value = value.reshape(h_dec, groups, 8, value.shape[1])
        turned = [pltpu.roll(value[:, g], 4, 1) for g in range(groups)]
        parts = [jnp.where(upper, turned[g], turned[g + 1]) for g in range(groups - 1)]
        return jnp.concatenate(parts, axis=1)

    for b in range(2):
        for par in range(2):
            v = part[b, par] + jnp.dot(up[b], c_d1[par, 12 * CH :], preferred_element_type=f32)
            v = silu(v)
            if par == 0:
                v = jnp.concatenate([v[:pairs] * top_scale, v[pairs:]], axis=0)
            else:
                v = jnp.concatenate([v[:-pairs], v[-pairs:] * bottom_scale], axis=0)
            both = jnp.concatenate([compact(v), compact(sides(v))], axis=2).astype(bf16)
            for i in range(h_dec):
                dec[2 * i + par, b * own : (b + 1) * own] = both[i]


def tail_body(tile_rows, own, dec, c_d2, c_out, last, put):
    n = tile_rows // TAIL_CHUNKS
    for i in range(TAIL_CHUNKS):
        windows = [
            dec[i * n + dy : (i + 1) * n + dy].reshape(n * 2 * own, 4 * CH) for dy in range(3)
        ]
        v = silu(
            jnp.dot(jnp.concatenate(windows, axis=1), c_d2[...], preferred_element_type=f32)
        )
        z = jnp.dot(v.astype(bf16), c_out[...], preferred_element_type=f32)
        z = z.reshape(n, 2 * own, 2 * CH)
        for px in range(2):
            for b in range(2):
                piece = z[:, b * own : (b + 1) * own, px * CH : (px + 1) * CH]
                last[pl.ds(i * n * own * 4 + 2 * px + b, n * own, stride=4), :] = piece.reshape(n * own, CH)
        put(i * n * own * 4, n * own * 4)


TAIL_CHUNKS = 1


def unet_scratch(tile_rows, tile_cols):
    line = 2 * pairs_of(tile_cols)
    half = line // 2
    h_pool = (tile_rows + 12) // 2
    return [
        pltpu.VMEM((2, 2, (tile_rows + 2 * HALO) * half, 2 * CH), bf16),
        pltpu.VMEM((2, 2, (tile_rows + 14) * half, 4 * CH), bf16),
        pltpu.VMEM((2, 2, 2, h_pool * half, 4 * CH), bf16),
        pltpu.VMEM((h_pool * line, CH), f32),
        pltpu.VMEM((h_pool * half, 4 * CH), f32),
        pltpu.VMEM(((h_pool - 2) * half, 4 * CH), f32),
        pltpu.VMEM((2, (h_pool - 5) * half, 6 * CH), bf16),
        pltpu.VMEM((2, 2, (h_pool - 5) * half, 2 * CH), f32),
    ]


def weight_scratch():
    square = pltpu.VMEM((12 * CH, 2 * CH), bf16)
    return [
        pltpu.VMEM((12 * FIELDS, 2 * CH), bf16), square, square, square,
        pltpu.VMEM((2, 18 * CH, 2 * CH), bf16),
    ]


def whole_kernel(tile_rows, tile_cols, *refs):
    ins, w_hbm, out_ref, scratch = refs[:4], refs[4:11], refs[11], refs[12:]
    w_vmem, w_sem, mats = scratch[:7], scratch[7], scratch[8:13]
    pad, own, unet_refs = scratch[13], scratch[14:34], scratch[34:-4]
    dec, c_d2, c_out, last = scratch[-4:]

    def weights_start():
        for i in range(7):
            pltpu.make_async_copy(w_hbm[i], w_vmem[i], w_sem.at[i]).start()

    def weights_ready():
        for i in range(7):
            pltpu.make_async_copy(w_hbm[i], w_vmem[i], w_sem.at[i]).wait()
        prepare(*w_vmem, *mats, c_d2, c_out)

    halo_here, sent = regrid_body(
        tile_rows, tile_cols, weights_start, weights_ready, *ins, pad, *own
    )
    row = lax.axis_index("row")
    unet_body(
        tile_rows, tile_cols, row == 0, row == lax.axis_size("row") - 1,
        halo_here, pad, mats, dec, *unet_refs,
    )

    def put(start, count):
        place = slice(start, start + count)
        out_ref[place, :] = last[place, :FIELDS].astype(bf16)

    tail_body(tile_rows, tile_cols // 2, dec, c_d2, c_out, last, put)
    sent()


def write_kernel(value, out_ref, sem):
    copy = pltpu.make_async_copy(value, out_ref, sem)
    copy.start()
    copy.wait()


def write(value):
    return pl.pallas_call(
        write_kernel,
        out_shape=jax.ShapeDtypeStruct(value.shape, bf16),
        in_specs=[pl.BlockSpec(memory_space=pltpu.VMEM)],
        out_specs=pl.BlockSpec(memory_space=pltpu.HBM),
        scratch_shapes=[pltpu.SemaphoreType.DMA],
    )(pltpu.with_memory_space_constraint(value, pltpu.VMEM))


EARLY = 0


def regrid_body(
    tile_rows, tile_cols, weights_start, weights_ready, src_in, req_in, sten_in, wgt_in, pad,
    src_ref, req_ref, sten_ref, wgt_ref, load, asks, reqs, src_t, mix, outbox, inbox, acc, slot_rows, weight_rows,
    req_send, req_recv, box_send, box_recv, halo_send, halo_recv,
):
    row, me = lax.axis_index("row"), lax.axis_index("col")
    n_row, n = lax.axis_size("row"), lax.axis_size("col")
    cap = req_ref.shape[1]
    cells = src_ref.shape[0]
    spots = tile_rows * tile_cols
    has_up, has_down = row > 0, row < n_row - 1
    wide = HALO // 2
    blocks = tile_cols // HALO
    edge = HALO * wide
    inner = tile_rows * wide

    loads = [
        pltpu.make_async_copy(outer, held, load.at[i])
        for i, (outer, held) in enumerate(
            [(req_in, req_ref), (src_in, src_ref), (sten_in, sten_ref), (wgt_in, wgt_ref)]
        )
    ]
    for copy in loads:
        copy.start()

    barrier = pltpu.get_barrier_semaphore()

    def greet(r, c):
        pl.semaphore_signal(
            barrier, inc=1, device_id=(r, lax.rem(c + n, n)), device_id_type=MESH
        )

    @pl.loop(1, n)
    def _(step):
        greet(row, me + step)

    @pl.when(has_up)
    def _():
        for d in (-1, 0, 1):
            greet(row - 1, me + d)

    @pl.when(has_down)
    def _():
        for d in (-1, 0, 1):
            greet(row + 1, me + d)

    weights_start()
    loads[0].wait()
    parts = cap // CH
    for j in range(n):
        for part in range(parts):
            asks[j, part : part + 1, :] = req_ref[j : j + 1, part * CH : (part + 1) * CH]

    rows_beside = jnp.minimum(row, 1) + jnp.minimum(n_row - 1 - row, 1)
    pl.semaphore_wait(barrier, n - 1 + 3 * rows_beside)

    def partner(step, sign):
        chip = lax.rem(me // 2 + sign * (step // 2) + n, n // 2)
        return chip * 2 + lax.rem(me + step, 2)

    def ask(step, sender):
        dest = partner(step, 1)
        return pltpu.make_async_remote_copy(
            src_ref=asks.at[dest],
            dst_ref=reqs.at[sender],
            send_sem=req_send.at[step],
            recv_sem=req_recv.at[sender],
            device_id=(row, dest),
            device_id_type=MESH,
        )

    @pl.loop(1, n)
    def _(i):
        ask(n - i, me).start()

    reqs[me] = asks[me]
    loads[1].wait()
    src_t[...] = src_ref[...].astype(f32).T.astype(bf16)

    loads[2].wait()
    loads[3].wait()
    taps = sten_ref.shape[0] // tile_rows
    lane = lax.broadcasted_iota(jnp.int32, (tile_cols, spots), 1)
    cell = lax.broadcasted_iota(jnp.int32, (tile_cols, spots), 0)
    column = lane // (spots // 2) + lane % wide * 2 + lane // inner % blocks * HALO
    turn = jnp.where(cell == column, 1.0, 0.0).astype(bf16)
    held = tile_rows * taps
    mine = lax.broadcasted_iota(jnp.int32, (held, spots), 0) // taps == (
        lax.broadcasted_iota(jnp.int32, (held, spots), 1) // wide % tile_rows
    )

    def in_order(values):
        spread = jnp.dot(values.astype(bf16), turn, preferred_element_type=f32)
        spread = jnp.where(mine, spread, 0.0).reshape(held // 8, 8, spots)
        total = jnp.sum(spread, axis=0)
        return total[:taps] + total[taps:]

    slots = sten_ref[...]
    slot_rows[...] = in_order((slots // 256).astype(f32)) * 256.0 + in_order((slots % 256).astype(f32))
    weight_rows[...] = in_order(wgt_ref[...])
    tile, piece = 16, 256

    def ladder(width):
        return lax.broadcasted_iota(jnp.int32, (tile, width), 0).astype(f32).astype(bf16)

    def spread(values):
        return jnp.broadcast_to(values, (tile, values.shape[1])).astype(bf16)

    lanes = min(512, spots)
    zero, one = jnp.zeros((), bf16), jnp.ones((), bf16)

    def mix_block(j):
        for left_lane in range(0, spots, lanes):
            here = slice(left_lane, left_lane + lanes)
            ids = ladder(lanes)
            weights = [spread(weight_rows[k : k + 1, here]) for k in range(taps)]
            for start in range(0, cap, piece):
                base = (j * cap + start).astype(f32)
                near = [spread(slot_rows[k : k + 1, here] - base) for k in range(taps)]
                for g in range(0, min(piece, cap), tile):
                    step_ids = ids + jnp.asarray(g, bf16)
                    total = None
                    for k in range(taps):
                        part = jnp.where(step_ids == near[k], weights[k], zero)
                        total = part if total is None else total + part
                    mix[j, start + g : start + g + tile, here] = total

    @pl.loop(0, EARLY)
    def _(j):
        mix_block(j)

    def picked(dest):
        asked = jnp.concatenate(
            [reqs[dest, part : part + 1, :] for part in range(parts)], axis=1
        ).astype(f32)
        ids = ladder(cap)
        rows = []
        for start in range(0, cells, piece):
            near = spread(asked - float(start))
            for g in range(0, piece, tile):
                rows.append(jnp.where(ids + jnp.asarray(g, bf16) == near, one, zero))
        hot = jnp.concatenate(rows, axis=0)
        return jnp.dot(src_t[...], hot, preferred_element_type=f32).astype(bf16)

    def post(step, sender, b):
        part = slice(b * FIELDS, (b + 1) * FIELDS)
        return pltpu.make_async_remote_copy(
            src_ref=outbox.at[step, part],
            dst_ref=inbox.at[sender, part],
            send_sem=box_send.at[b, step],
            recv_sem=box_recv.at[b, sender],
            device_id=(row, partner(step, 1)),
            device_id_type=MESH,
        )

    @pl.loop(1, n)
    def _(i):
        step = n - i
        dest = partner(step, 1)
        ask(step, dest).wait_recv()
        outbox[step] = picked(dest)
        post(step, me, 0).start()

    @pl.loop(1, n)
    def _(i):
        post(n - i, me, 1).start()

    inbox[me] = picked(me)

    @pl.loop(EARLY, n)
    def _(j):
        mix_block(j)

    def gather(b):
        part = slice(b * FIELDS, (b + 1) * FIELDS)
        post(1, partner(1, -1), b).wait_recv()
        total = jnp.dot(inbox[me, part], mix[me], preferred_element_type=f32)
        beside = partner(1, -1)
        acc[...] = total + jnp.dot(inbox[beside, part], mix[beside], preferred_element_type=f32)

        @pl.loop(1, n // 2)
        def _(i):
            senders = []
            for step in (n - 2 * i + 1, n - 2 * i):
                sender = partner(step, -1)
                post(step, sender, b).wait_recv()
                senders.append(sender)
            left, right = [
                jnp.dot(inbox[sender, part], mix[sender], preferred_element_type=f32)
                for sender in senders
            ]
            acc[...] += left + right

        turned = jnp.concatenate([acc[:, : spots // 2], acc[:, spots // 2 :]], axis=0).T.astype(bf16)
        for xb in range(blocks):
            pad[b, xb + 1, edge : edge + inner] = turned[xb * inner : (xb + 1) * inner]

        @pl.when(jnp.logical_not(has_up))
        def _():
            pad[b, :, :edge] = jnp.zeros((blocks + 2, edge, CH), bf16)

        @pl.when(jnp.logical_not(has_down))
        def _():
            pad[b, :, edge + inner :] = jnp.zeros((blocks + 2, edge, CH), bf16)

    mid = slice(edge, edge + inner)
    first, last = slice(edge, 2 * edge), slice(inner, inner + edge)
    low, high = slice(0, edge), slice(edge + inner, 2 * edge + inner)
    every = slice(1, blocks + 1)
    left, right = slice(1, 2), slice(blocks, blocks + 1)
    before, after = slice(0, 1), slice(blocks + 1, blocks + 2)
    moves = [
        (0, 1, (right, mid), (before, mid)),
        (0, -1, (left, mid), (after, mid)),
        (1, 0, (every, last), (every, low)),
        (1, 1, (right, last), (before, low)),
        (1, -1, (left, last), (after, low)),
        (-1, 0, (every, first), (every, high)),
        (-1, 1, (right, first), (before, high)),
        (-1, -1, (left, first), (after, high)),
    ]

    def shift(i, b):
        dr, dc, src, dst = moves[i]
        return pltpu.make_async_remote_copy(
            src_ref=pad.at[b, src[0], src[1]],
            dst_ref=pad.at[b, dst[0], dst[1]],
            send_sem=halo_send.at[b, i],
            recv_sem=halo_recv.at[b, i],
            device_id=(row + dr, lax.rem(me + dc + n, n)),
            device_id_type=MESH,
        )

    def halo_start(b):
        @pl.when(has_down)
        def _():
            for i in (2, 3, 4):
                shift(i, b).start()

        @pl.when(has_up)
        def _():
            for i in (5, 6, 7):
                shift(i, b).start()

        for i in (0, 1):
            shift(i, b).start()

    def halo_here(b):
        for i in (0, 1):
            shift(i, b).wait_recv()

        @pl.when(has_up)
        def _():
            for i in (2, 3, 4):
                shift(i, b).wait_recv()

        @pl.when(has_down)
        def _():
            for i in (5, 6, 7):
                shift(i, b).wait_recv()

    def sent():
        @pl.loop(1, n)
        def _(step):
            ask(step, me).wait_send()
            for b in range(2):
                post(step, me, b).wait_send()

        for b in range(2):
            for i in (0, 1):
                shift(i, b).wait_send()

        @pl.when(has_down)
        def _():
            for b in range(2):
                for i in (2, 3, 4):
                    shift(i, b).wait_send()

        @pl.when(has_up)
        def _():
            for b in range(2):
                for i in (5, 6, 7):
                    shift(i, b).wait_send()

    gather(0)
    halo_start(0)
    weights_ready()
    gather(1)
    halo_start(1)
    return halo_here, sent


def forward(source, wanted, stencil, weight, weights, tile_rows, tile_cols):
    n, cap = wanted.shape
    cells, columns = source.shape
    spots = tile_rows * tile_cols
    blocks = tile_cols // HALO
    rows = tile_rows + 2 * HALO
    taps = stencil.shape[0] // tile_rows
    dma = pltpu.SemaphoreType.DMA
    return pl.pallas_call(
        functools.partial(whole_kernel, tile_rows, tile_cols),
        out_shape=pltpu.VMEM((2 * spots, FIELDS), bf16),
        in_specs=[pl.BlockSpec(memory_space=pltpu.HBM)] * 11,
        out_specs=pl.BlockSpec(memory_space=pltpu.VMEM),
        scratch_shapes=[pltpu.VMEM(w.shape, bf16) for w in weights]
        + [dma((7,))]
        + weight_scratch()
        + [
            pltpu.VMEM((2, blocks + 2, rows * HALO // 2, columns), bf16),
            pltpu.VMEM(source.shape, bf16),
            pltpu.VMEM(wanted.shape, jnp.int32),
            pltpu.VMEM(stencil.shape, jnp.int32),
            pltpu.VMEM(weight.shape, f32),
            dma((4,)),
            pltpu.VMEM((n, cap // CH, CH), jnp.int32),
            pltpu.VMEM((n, cap // CH, CH), jnp.int32),
            pltpu.VMEM((columns, cells), bf16),
            pltpu.VMEM((n, cap, spots), bf16),
            pltpu.VMEM((n, columns, cap), bf16),
            pltpu.VMEM((n, columns, cap), bf16),
            pltpu.VMEM((FIELDS, spots), f32),
            pltpu.VMEM((taps, spots), f32),
            pltpu.VMEM((taps, spots), f32),
            dma((n,)), dma((n,)), dma((2, n)), dma((2, n)), dma((2, 8)), dma((2, 8)),
        ]
        + unet_scratch(tile_rows, tile_cols)
        + [
            pltpu.VMEM((tile_rows + 2, tile_cols, 4 * CH), bf16),
            pltpu.VMEM((12 * CH, 2 * CH), bf16),
            pltpu.VMEM((2 * CH, 2 * CH), bf16),
            pltpu.VMEM((2 * spots, CH), f32),
        ],
        compiler_params=pltpu.CompilerParams(
            collective_id=0, has_side_effects=True, vmem_limit_bytes=40 * 1024 * 1024
        ),
        cost_estimate=pl.CostEstimate(
            flops=10**9, bytes_accessed=2 * 10**6, transcendentals=0
        ),
    )(*[pltpu.with_memory_space_constraint(a, pltpu.HBM) for a in (source, wanted, stencil, weight, *weights)])


def body(source_tiles, requests, stencil, regrid_weight, *weights):
    tile_rows, tile_cols, taps = stencil.shape
    cells, columns = source_tiles.shape[2:]
    done = forward(
        source_tiles.reshape(cells, columns),
        requests.reshape(requests.shape[2:]),
        stencil.transpose(0, 2, 1).reshape(tile_rows * taps, tile_cols),
        regrid_weight.transpose(0, 2, 1).reshape(tile_rows * taps, tile_cols),
        (*weights[:-1], weights[-1].T),
        tile_rows,
        tile_cols,
    )
    return write(done).reshape(tile_rows, tile_cols, 2, FIELDS)


def solution(mesh):
    placed = (P("row", "col", None, None),) * 2 + (P("row", "col", None),) * 2 + (P(),) * 7
    return jax.shard_map(
        body, mesh=mesh, in_specs=placed, out_specs=P("row", "col", None, None), check_vma=False
    )
```
